256 devices in a mesh: seq: 64 (over z, y, core), mp: 4 (over x).
Axes of the slice: x: 4, y: 4, z: 8, core: 2. Of those that a mesh axis runs over, the one named last changes fastest.
Arguments:
- se_query: bfloat16 [8192, 8192], P('seq', 'mp'), may hold values from -6 to 6
- se_key: bfloat16 [8192, 8192], P('seq', 'mp'), may hold values from -6 to 6
- se_value: bfloat16 [8192, 8192], P('seq', 'mp'), may hold values from -6 to 6
- mr_query: bfloat16 [8192, 8192], P('seq', 'mp'), may hold values from -6 to 6
- mr_key: bfloat16 [8192, 8192], P('seq', 'mp'), may hold values from -6 to 6
- att_query: bfloat16 [8192, 8192], P('seq', 'mp'), may hold values from -52 to 52
- att_key: bfloat16 [8192, 8192], P('seq', 'mp'), may hold values from -6 to 6
- doc_ids: int32 [8192], P('seq'), may hold values from 0 to 127, never falling along the last dimension, each value on 1 to 1024 neighbouring positions
- se_taps: float32 [7, 8192], P(None, 'mp'), may hold values from -2.4 to 2.4
- mr_taps: bfloat16 [128, 8192], P(None, 'mp'), may hold values from -1.796875 to 1.796875
- mr_rates: float32 [8192], P('mp'), may hold values from 0.003 to 0.1
- se_gain: float32 [8192], P('mp'), may hold values from 0.1 to 1.9
- mr_gain: float32 [8192], P('mp'), may hold values from 0.1 to 1.9
- att_gain: float32 [8192], P('mp'), may hold values from 0.1 to 1.9
Outputs:
- mr_out: bfloat16 [8192, 8192], P('seq', 'mp')
- att_out: bfloat16 [8192, 8192], P('seq', 'mp')
The draws below stay inside these ranges and needn't reach their ends.
Inputs may be any that keep to these rules, and one draw needn't show every extreme that they name: `doc_ids`: document ids never fall along the pack; each document has 1 to 1024 tokens and one has exactly 1024.
All inputs are finite; a program needn't handle non-finite values.
Results may differ from the reference program's by a relative error of at most 0.017.
Values may be sent and summed in bfloat16 or wider, within the bound.
A program may use at most 64 MiB of HBM per device.

```python
import math
import jax
import jax.numpy as jnp
import numpy as np
from jax import lax

D = 8192
HEADS = 64
HEAD_DIM = 128
SE_TAPS = 7
MR_TAPS = 128
TOK_DEV = 128
TOKENS = 8192
REACH = 8
DOC_MOST = 1024
DOCS = 128


def shared_keys(key, copy_amp):
    normal_part = jnp.clip(jax.random.normal(jax.random.fold_in(key, 11), (TOKENS, D), jnp.float32), -6.0, 6.0)
    base = normal_part
    positions = jnp.arange(TOKENS)
    before_mark = (positions + 1) % 97 == 50
    following = jnp.roll(base, -1, axis=0)
    return jnp.where(before_mark[:, None] & (copy_amp > 0.0), following, base)


def draw_att_key(key, part):
    values = shared_keys(key, 0.0)
    return values.astype(jnp.bfloat16)


def draw_att_query(key, part):
    key = jax.random.fold_in(key, 7)
    values = jnp.clip(jax.random.normal(key, (TOKENS, D), jnp.float32), -6.0, 6.0)
    return values.astype(jnp.bfloat16)


def levels(own_key, shape, split, smallest, largest):
    def one(axis_at, shards_of):
        steps = jax.random.uniform(jax.random.fold_in(jax.random.fold_in(own_key, 6), axis_at), (shards_of,), jnp.float32, smallest / len(split), largest / len(split))
        return jnp.repeat(jnp.exp(steps), shape[axis_at] // shards_of).reshape((-1,) + (1,) * (len(shape) - axis_at - 1))

    level = one(*split[0])
    for cut in split[1:]:
        level = level * one(*cut)
    return level


def profile(number_of, total, most, lean):
    weights = [(1 << 20) // math.isqrt(grade ** lean) + 1 for grade in range(2, number_of + 1)]
    surplus, holding = total - most - (number_of - 1), [1] * (number_of - 1)
    while surplus > 0:
        movable = [i for i in range(number_of - 1) if holding[i] < most]
        pool, left = sum([weights[i] for i in movable]), surplus
        for i in movable:
            extra = min(most - holding[i], max(1, left * weights[i] // pool), surplus)
            holding[i] = holding[i] + extra
            surplus = surplus - extra
    return np.array([most] + holding)


def ragged(stream_key, amount, total, bound, lean):
    if amount == 2:
        one = jax.random.randint(stream_key, (), max(1, total - bound), min(bound, total - 1) + 1)
        return jnp.stack([one, total - one])
    tallies = jnp.asarray(profile(amount, total, bound, lean), jnp.int32)
    couples = (amount - 1) // 2
    giver, receiver = tallies[1:1 + 2 * couples:2], tallies[2:2 + 2 * couples:2]
    room = jnp.minimum(giver - 1, bound - receiver)
    moved = jax.random.randint(jax.random.fold_in(stream_key, 1), (couples,), 0, 1 << 20) % (room + 1)
    tallies = tallies.at[1:1 + 2 * couples:2].set(giver - moved).at[2:2 + 2 * couples:2].set(receiver + moved)
    return tallies[jax.random.permutation(jax.random.fold_in(stream_key, 2), amount)]


def scatter_about(stream_key, extent, width, bound, shards=(), held_as=jnp.bfloat16):
    drawn = jax.random.normal(stream_key, extent, jnp.float32) * width
    if len(shards) > 0:
        drawn = levels(stream_key, extent, shards, -0.22, 0.18) * drawn
    return jnp.clip(drawn, min=-bound, max=bound).astype(held_as)


def setup_inputs(seed: int = 0) -> dict:
    arg_keys = jax.random.split(jax.random.key(seed), 15)
    return {
        "se_query": scatter_about(arg_keys[0], (TOKENS, D), 1.0, 6.0, ((0, 64), (1, 4))),
        "se_key": scatter_about(arg_keys[1], (TOKENS, D), 1.0, 6.0, ((0, 64), (1, 4))),
        "se_value": scatter_about(arg_keys[2], (TOKENS, D), 1.0, 6.0, ((0, 64), (1, 4))),
        "mr_query": scatter_about(arg_keys[3], (TOKENS, D), 1.0, 6.0, ((0, 64), (1, 4))),
        "mr_key": scatter_about(arg_keys[4], (TOKENS, D), 1.0, 6.0, ((0, 64), (1, 4))),
        "att_query": draw_att_query(jax.random.fold_in(arg_keys[14], 71), 0),
        "att_key": draw_att_key(jax.random.fold_in(arg_keys[14], 71), 0),
        "doc_ids": jnp.searchsorted(jnp.cumsum(ragged(arg_keys[7], DOCS, TOKENS, DOC_MOST, 2)), jnp.arange(TOKENS), side="right").astype(jnp.int32),
        "se_taps": scatter_about(arg_keys[8], (SE_TAPS, D), 0.4, 2.4, ((1, 4),), jnp.float32),
        "mr_taps": scatter_about(arg_keys[9], (MR_TAPS, D), 0.3, 1.796875, ((1, 4),)),
        "mr_rates": jnp.clip(jnp.exp(math.log(0.1) - 3.506558 * jax.random.uniform(arg_keys[10], (D,), jnp.float32) ** levels(arg_keys[10], (D,), ((0, 4),), -0.2, 0.2)), 0.003, 0.1),
        "se_gain": jnp.clip(1.0 + 0.18 * jax.random.normal(arg_keys[11], (D,), jnp.float32), 0.1, 1.9),
        "mr_gain": jnp.clip(1.0 + 0.18 * jax.random.normal(arg_keys[12], (D,), jnp.float32), 0.1, 1.9),
        "att_gain": jnp.clip(1.0 + 0.18 * jax.random.normal(arg_keys[13], (D,), jnp.float32), 0.1, 1.9),
    }


def causal_filter(signal, doc_ids, taps):
    tap_count = taps.shape[0]
    row_count, channels = signal.shape
    extended = jnp.concatenate([jnp.zeros((tap_count - 1, channels), signal.dtype), signal], 0)
    ext_ids = jnp.concatenate([jnp.full((tap_count - 1,), -1, jnp.int32), doc_ids.astype(jnp.int32)], 0)

    def add_tap(tap_index, running):
        start = (tap_count - 1 - tap_index).astype(jnp.int32)
        window_rows = lax.dynamic_slice_in_dim(extended, start, row_count, 0).astype(jnp.float32)
        window_ids = lax.dynamic_slice_in_dim(ext_ids, start, row_count, 0)
        tap_row = lax.dynamic_index_in_dim(taps, tap_index, 0, keepdims=False).astype(jnp.float32)
        return running + jnp.where((window_ids == doc_ids)[:, None], window_rows * tap_row[None, :], 0.0)
    return lax.fori_loop(0, tap_count, add_tap, jnp.zeros((row_count, channels), jnp.float32))

def attention(att_query, att_key, att_value, doc_ids):
    reach_rows = REACH * TOK_DEV
    key_pad = jnp.concatenate([jnp.zeros((reach_rows, D), att_key.dtype), att_key], 0)
    value_pad = jnp.concatenate([jnp.zeros((reach_rows, D), att_value.dtype), att_value], 0)
    ids_pad = jnp.concatenate([jnp.full((reach_rows,), -1, jnp.int32), doc_ids.astype(jnp.int32)], 0)
    score_scale = HEAD_DIM ** (-0.5)

    def one_block(block_index):
        start = (block_index * TOK_DEV).astype(jnp.int32)
        queries = lax.dynamic_slice_in_dim(att_query, start, TOK_DEV, 0).astype(jnp.float32)
        query_ids = lax.dynamic_slice_in_dim(doc_ids.astype(jnp.int32), start, TOK_DEV, 0)
        key_rows = lax.dynamic_slice_in_dim(key_pad, start, reach_rows + TOK_DEV, 0).astype(jnp.float32)
        value_rows = lax.dynamic_slice_in_dim(value_pad, start, reach_rows + TOK_DEV, 0).astype(jnp.float32)
        key_ids = lax.dynamic_slice_in_dim(ids_pad, start, reach_rows + TOK_DEV, 0)
        query_pos = jnp.arange(TOK_DEV)[:, None]
        key_pos = jnp.arange(reach_rows + TOK_DEV)[None, :] - reach_rows
        allowed = (query_ids[:, None] == key_ids[None, :]) & (key_pos <= query_pos)
        queries = queries.reshape(TOK_DEV, HEADS, HEAD_DIM)
        key_rows = key_rows.reshape(-1, HEADS, HEAD_DIM)
        value_rows = value_rows.reshape(-1, HEADS, HEAD_DIM)
        scores = jnp.einsum('qhd,khd->hqk', queries, key_rows) * score_scale
        scores = jnp.where(allowed[None], scores, -1e+30)
        row_max = lax.optimization_barrier(jnp.max(scores, axis=2, keepdims=True))
        expo = jnp.where(allowed[None], jnp.exp(scores - row_max), 0.0)
        denom = lax.optimization_barrier(jnp.sum(expo, axis=2, keepdims=True))
        weights = (expo / denom).astype(jnp.bfloat16)
        mixed = jnp.einsum('hqk,khd->qhd', weights.astype(jnp.float32), value_rows)
        return mixed.reshape(TOK_DEV, D)
    blocks = lax.map(one_block, jnp.arange(TOKENS // TOK_DEV, dtype=jnp.int32))
    return blocks.reshape(TOKENS, D)

def width_norm(layer_out, gain):
    mean_square = lax.optimization_barrier(jnp.sum(layer_out * layer_out, axis=1)) / D
    return (layer_out * lax.rsqrt(mean_square + 1e-06)[:, None] * gain[None, :]).astype(jnp.bfloat16)

def reference(se_query, se_key, se_value, mr_query, mr_key, att_query, att_key, doc_ids, se_taps, mr_taps, mr_rates, se_gain, mr_gain, att_gain):
    se_u = (se_key.astype(jnp.float32) * se_value.astype(jnp.float32)).astype(jnp.bfloat16)
    se_y = se_query.astype(jnp.float32) * causal_filter(se_u, doc_ids, se_taps)
    se_out = width_norm(se_y, se_gain)
    mr_u = (mr_key.astype(jnp.float32) * se_out.astype(jnp.float32)).astype(jnp.bfloat16)
    tap_pos = jnp.arange(MR_TAPS).astype(jnp.float32)[:, None]
    mr_filter = mr_taps.astype(jnp.float32) * jnp.exp(-mr_rates[None, :] * tap_pos)
    mr_y = mr_query.astype(jnp.float32) * causal_filter(mr_u, doc_ids, mr_filter)
    mr_out = width_norm(mr_y, mr_gain)
    att_y = attention(att_query, att_key, mr_out, doc_ids)
    return (mr_out, width_norm(att_y, att_gain))
```

```python
import functools
import math

import jax
import jax.numpy as jnp
from jax import lax
from jax.experimental import pallas as pl
from jax.experimental.pallas import tpu as pltpu
from jax.sharding import PartitionSpec as P

D = 8192
HEAD = 128
TOK = 128
SE_K = 7
MR_K = 128
MESH = pl.DeviceIdType.MESH
F32 = jnp.float32
BF16 = jnp.bfloat16


def ring(index, step, size):
    return lax.rem(index + (step + size), size)


def kernel(
    planes,
    width,
    mps,
    d_model,
    se_q,
    se_k,
    se_v,
    mr_q,
    mr_k,
    att_q,
    att_k,
    ids,
    se_taps,
    mr_taps,
    rates,
    se_gain,
    mr_gain,
    att_gain,
    mr_out,
    att_out,
    ue,
    ybuf,
    filt,
    idc,
    m7,
    ma,
    mb,
    um,
    ul,
    sq,
    sh_send,
    sh_recv,
    v_send,
    v_recv,
    r_send,
    r_recv,
    ps_send,
    ps_recv,
    id_send,
    id_prev,
    id_all,
    k_all,
    q_all,
    v_all,
    s_buf,
    p_all,
    linv,
    o_send,
    o_all,
    loc_sem,
    k_ss,
    k_rs,
    q_ss,
    q_rs,
    v_ss,
    v_rs,
    o_ss,
    o_rs,
    i_ss,
    i_rs,
    f_ss,
    f_rs,
    ps_ss,
    ps_rs,
    h_ss,
    h_rs,
):
    seq = lax.axis_index("seq")
    mp = lax.axis_index("mp")
    count = planes * width
    z = seq // width
    w = lax.rem(seq, width)
    chans = se_q.shape[1]
    groups = chans // 128
    cw = chans // width
    heads = cw // HEAD
    span = width + 1

    def mate(step):
        return z * width + ring(w, step, width)

    def remote(src, dst, ss, rs, where):
        return pltpu.make_async_remote_copy(
            src_ref=src, dst_ref=dst, send_sem=ss, recv_sem=rs, device_id=where, device_id_type=MESH
        )

    def lanes(g, size=128):
        return pl.ds(pl.multiple_of(g * size, 128), size)

    next_seq = {"seq": ring(seq, 1, count)}
    next_plane = {"seq": ring(seq, width, count)}

    barrier = pltpu.get_barrier_semaphore()
    for step in range(1, width):
        pl.semaphore_signal(barrier, inc=1, device_id={"seq": mate(step)}, device_id_type=MESH)
    pl.semaphore_signal(barrier, inc=1, device_id={"seq": ring(seq, -width, count)}, device_id_type=MESH)
    pl.semaphore_signal(barrier, inc=1, device_id={"seq": ring(seq, -1, count)}, device_id_type=MESH)
    for step in range(1, mps):
        pl.semaphore_signal(barrier, inc=1, device_id={"mp": ring(mp, step, mps)}, device_id_type=MESH)

    own_k = pltpu.make_async_copy(att_k.at[:, lanes(w, cw)], k_all.at[width + w], loc_sem.at[0])
    own_q = pltpu.make_async_copy(att_q.at[:, lanes(w, cw)], q_all.at[w], loc_sem.at[1])
    own_k.start()
    own_q.start()

    id_row = ids[...].astype(F32)
    id_send[...] = jnp.broadcast_to(id_row, (8, 128))
    id_all[width + w] = jnp.broadcast_to(id_row, (8, 128))
    idc[TOK:] = jnp.broadcast_to(id_row, (TOK, 128)).T
    sh_send[...] = (se_k[TOK - 16 :, :].astype(F32) * se_v[TOK - 16 :, :].astype(F32)).astype(BF16)

    pl.semaphore_wait(barrier, (width - 1) + 2 + (mps - 1))

    id_next = remote(id_send, id_prev, h_ss.at[0], h_rs.at[0], next_seq)
    id_next.start()
    sh_next = remote(sh_send, sh_recv, h_ss.at[1], h_rs.at[1], next_seq)
    sh_next.start()
    sends = [id_next, sh_next]
    for step in range(1, width):
        there = ring(w, step, width)
        copy = remote(
            id_send, id_all.at[width + w], i_ss.at[step], i_rs.at[w], {"seq": mate(step)}
        )
        copy.start()
        sends.append(copy)
        copy = remote(
            att_k.at[:, lanes(there, cw)],
            k_all.at[width + w],
            k_ss.at[step],
            k_rs.at[w],
            {"seq": mate(step)},
        )
        copy.start()
        sends.append(copy)

    def local_part(g, carry):
        col = lanes(g)
        row = lax.broadcasted_iota(jnp.int32, (MR_K, 128), 0).astype(F32)
        filt[:, col] = mr_taps[:, col].astype(F32) * jnp.exp(-(rates[:, col] * row))
        ue[TOK:, col] = (
            (se_k[:, col].astype(F32) * se_v[:, col].astype(F32)).astype(BF16).astype(F32)
        )
        return carry

    lax.fori_loop(0, groups, local_part, 0)

    id_next.wait_recv()
    idc[:TOK] = jnp.broadcast_to(id_prev[0:1, :], (TOK, 128)).T
    here = idc[TOK:]
    for tap in range(1, SE_K):
        m7[tap] = (idc[TOK - tap : 2 * TOK - tap] == here).astype(F32)

    sh_next.wait_recv()
    ue[TOK - 8 : TOK, :] = sh_recv[...].astype(F32)[8:16, :]
    sq[...] = jnp.zeros_like(sq)

    def short_part(g, carry):
        col = lanes(g)
        for rb in range(TOK // 32):
            rows = slice(32 * rb, 32 * rb + 32)
            acc = ue[TOK + 32 * rb : TOK + 32 * rb + 32, col] * se_taps[0:1, col]
            for tap in range(1, SE_K):
                acc += (
                    ue[TOK + 32 * rb - tap : TOK + 32 * rb + 32 - tap, col] * m7[tap, rows, :]
                ) * se_taps[tap : tap + 1, col]
            out = se_q[rows, col].astype(F32) * acc
            sq[rows, :] += out * out
            out = out * se_gain[:, col]
            ybuf[rows, col] = out
            v_send[rows, col] = (out * mr_k[rows, col].astype(F32)).astype(BF16)
        return carry

    parts = 4
    per = groups // parts
    halo = []
    for part in range(parts):
        lax.fori_loop(part * per, (part + 1) * per, short_part, 0)
        cols = slice(part * per * 128, (part + 1) * per * 128)
        copy = remote(
            v_send.at[:, cols], v_recv.at[:, cols], h_ss.at[3 + part], h_rs.at[3 + part], next_seq
        )
        copy.start()
        halo.append(copy)
    sends += halo

    def psum_start(which):
        row = jnp.sum(sq[...].T, axis=0, keepdims=True)
        ps_send[which] = jnp.broadcast_to(row, (8, 128))
        copies = []
        for step in range(1, mps):
            copy = remote(
                ps_send.at[which],
                ps_recv.at[which, step],
                ps_ss.at[which, step],
                ps_rs.at[which, step],
                {"mp": ring(mp, step, mps)},
            )
            copy.start()
            copies.append(copy)
        return copies

    def psum_end(which, copies):
        total = ps_send[which]
        for step, copy in enumerate(copies, 1):
            copy.wait_recv()
            total = total + ps_recv[which, step]
        return lax.rsqrt(total / d_model + 1e-06)

    def column(rows8):
        return jnp.broadcast_to(rows8[0:1, :], (TOK, 128)).T

    copies = psum_start(0)
    sends += copies

    blocks = TOK // 16

    def masks(a, carry):
        base = pl.multiple_of(a * 16, 16)
        first = idc[pl.ds(base + TOK, 8), :][0:1, :]
        win = idc[pl.ds(base, TOK + 16), :]
        ma[a] = (win == first).astype(F32)
        ul[...] = idc[pl.ds(base + TOK - 16, 32), :]
        sub = lax.broadcasted_iota(jnp.int32, (8, 128), 0)
        at = 0
        for tile in range(2):
            mine = ul[16 + 8 * tile : 24 + 8 * tile, :]
            for tap in range(8 * tile + 8):
                then = ul[16 + 8 * tile - tap : 24 + 8 * tile - tap, :]
                keep = (mine == then) & (mine != first) & (sub + 8 * tile >= tap)
                mb[a, at] = keep.astype(F32)
                at += 1
        return carry

    lax.fori_loop(0, blocks, masks, 0)

    r_own = psum_end(0, copies)
    r_send[...] = r_own
    r_next = remote(r_send, r_recv, h_ss.at[2], h_rs.at[2], next_seq)
    r_next.start()
    sends.append(r_next)
    idc[:TOK] = column(r_own)

    own_k.wait()
    for step in range(1, width):
        src = ring(w, -step, width)
        remote(
            k_all.at[width + src], k_all.at[width + src], k_ss.at[step], k_rs.at[src], next_seq
        ).wait_recv()
        remote(
            id_all.at[width + src], id_all.at[width + src], i_ss.at[step], i_rs.at[src], next_seq
        ).wait_recv()
    k_next = remote(
        k_all.at[pl.ds(width, width)], k_all.at[pl.ds(0, width)], f_ss.at[width], f_rs.at[width], next_plane
    )
    k_next.start()
    i_next = remote(
        id_all.at[pl.ds(width, width)],
        id_all.at[pl.ds(0, width)],
        f_ss.at[width + 1],
        f_rs.at[width + 1],
        next_plane,
    )
    i_next.start()
    sends += [k_next, i_next]
    for step in range(1, width):
        there = ring(w, step, width)
        copy = remote(
            att_q.at[:, lanes(there, cw)], q_all.at[w], q_ss.at[step], q_rs.at[w], {"seq": mate(step)}
        )
        copy.start()
        sends.append(copy)

    r_next.wait_recv()
    idc[TOK:] = column(r_recv[...])
    for copy in halo:
        copy.wait_recv()
    sq[...] = jnp.zeros_like(sq)

    def medium_part(g, carry):
        col = lanes(g)
        se_out = (ybuf[:, col] * idc[:TOK]).astype(BF16).astype(F32)
        ue[TOK:, col] = (mr_k[:, col].astype(F32) * se_out).astype(BF16).astype(F32)
        ue[:TOK, col] = v_recv[:, col].astype(F32) * idc[TOK:]

        def block(a, carry):
            base = pl.multiple_of(a * 16, 16)
            um[...] = ue[pl.ds(base, TOK + 16), col] * ma[a]
            ul[...] = ue[pl.ds(base + TOK - 16, 32), col]
            acc = [[jnp.zeros((8, 128), F32) for _ in range(4)] for _ in range(2)]
            for phase in range(8):
                wins = {k: um[8 * k - phase : 8 * k - phase + 8, :] for k in range(1, 18)}
                for m in range(MR_K // 8):
                    tap = filt[8 * m + phase : 8 * m + phase + 1, col]
                    for tile in range(2):
                        acc[tile][phase % 4] += wins[16 + tile - m] * tap
            at = 0
            for tile in range(2):
                total = (acc[tile][0] + acc[tile][1]) + (acc[tile][2] + acc[tile][3])
                total = total * ma[a, TOK + 8 * tile : TOK + 8 * tile + 8, :]
                for tap in range(8 * tile + 8):
                    total += (ul[16 + 8 * tile - tap : 24 + 8 * tile - tap, :] * mb[a, at]) * filt[
                        tap : tap + 1, col
                    ]
                    at += 1
                um[8 * tile : 8 * tile + 8, :] = total
            rows = pl.ds(base, 16)
            out = mr_q[rows, col].astype(F32) * um[0:16, :]
            ybuf[rows, col] = out
            sq[rows, :] += out * out
            return carry

        return lax.fori_loop(0, blocks, block, carry)

    lax.fori_loop(0, groups, medium_part, 0)

    copies = psum_start(1)
    sends += copies
    r_own = psum_end(1, copies)
    idc[:TOK] = column(r_own)

    def norm_chunk(there):
        for part in range(cw // 128):
            col = lanes(there * (cw // 128) + part)
            mr_out[:, col] = (ybuf[:, col] * idc[:TOK] * mr_gain[:, col]).astype(BF16)

    for step in range(1, width):
        there = ring(w, step, width)
        norm_chunk(there)
        copy = remote(
            mr_out.at[:, lanes(there, cw)],
            v_all.at[width + w],
            v_ss.at[step],
            v_rs.at[w],
            {"seq": mate(step)},
        )
        copy.start()
        sends.append(copy)
    norm_chunk(w)
    own_v = pltpu.make_async_copy(mr_out.at[:, lanes(w, cw)], v_all.at[width + w], loc_sem.at[2])
    own_v.start()

    own_q.wait()
    for step in range(1, width):
        src = ring(w, -step, width)
        remote(q_all.at[src], q_all.at[src], q_ss.at[step], q_rs.at[src], next_seq).wait_recv()
    k_next.wait_recv()
    i_next.wait_recv()

    scale = HEAD**-0.5 * math.log2(math.e)
    tri = lax.broadcasted_iota(jnp.int32, (TOK, TOK), 0) >= lax.broadcasted_iota(
        jnp.int32, (TOK, TOK), 1
    )

    def weights(b):
        id_q = column(id_all[width + b])
        for h in range(heads):
            hl = slice(h * HEAD, (h + 1) * HEAD)
            q = q_all[b, :, hl]
            top = None
            for kk in range(span):
                s = lax.dot_general(
                    q,
                    k_all[b + kk, :, hl],
                    (((1,), (1,)), ((), ())),
                    preferred_element_type=F32,
                )
                keep = id_q == jnp.broadcast_to(id_all[b + kk][0:1, :], (TOK, TOK))
                if kk == span - 1:
                    keep = keep & tri
                s = jnp.where(keep, s * scale, -1e30)
                s_buf[kk] = s
                top = s if top is None else jnp.maximum(top, s)
            top = jnp.max(top, axis=1, keepdims=True)
            total = None
            for kk in range(span):
                e = jnp.exp2(s_buf[kk] - top)
                total = e if total is None else total + e
                p_all[b, h, :, kk * TOK : (kk + 1) * TOK] = e.astype(BF16)
            total = jnp.sum(total, axis=1, keepdims=True)
            linv[b, h] = jnp.broadcast_to(1.0 / total, (TOK, TOK))

    own_v.wait()

    def weigh_and_forward(i, carry):
        weights(i)
        j = width - 1 - i

        @pl.when(j != w)
        def _():
            remote(
                v_all.at[width + j], v_all.at[width + j], v_ss.at[0], v_rs.at[j], next_seq
            ).wait_recv()

        remote(v_all.at[width + j], v_all.at[j], f_ss.at[j], f_rs.at[j], next_plane).start()
        return carry

    lax.fori_loop(0, width, weigh_and_forward, 0)

    def mix(i, carry):
        b = width - 1 - i
        remote(v_all.at[width + b], v_all.at[b], f_ss.at[b], f_rs.at[b], next_plane).wait_recv()
        for h in range(heads):
            hl = slice(h * HEAD, (h + 1) * HEAD)
            o = None
            for kk in range(span):
                term = lax.dot_general(
                    p_all[b, h, :, kk * TOK : (kk + 1) * TOK],
                    v_all[b + kk, :, hl],
                    (((1,), (0,)), ((), ())),
                    preferred_element_type=F32,
                )
                o = term if o is None else o + term
            o_send[b, :, hl] = (o * linv[b, h]).astype(BF16)

        @pl.when(b != w)
        def _():
            remote(
                o_send.at[b],
                o_all.at[w],
                o_ss.at[b],
                o_rs.at[w],
                {"seq": z * width + b},
            ).start()

        return carry

    lax.fori_loop(0, width, mix, 0)
    o_all[w] = o_send[w]
    sq[...] = jnp.zeros_like(sq)

    def collect(i, carry):
        src = ring(w, i, width)

        @pl.when(i != 0)
        def _():
            remote(o_all.at[src], o_all.at[src], o_ss.at[src], o_rs.at[src], next_seq).wait_recv()

        for part in range(cw // 128):
            out = o_all[src, :, part * 128 : (part + 1) * 128].astype(F32)
            sq[...] += out * out
        return carry

    lax.fori_loop(0, width, collect, 0)
    copies = psum_start(2)
    sends += copies
    scale_col = column(psum_end(2, copies))

    for j in range(width):
        for part in range(cw // 128):
            col = slice(j * cw + part * 128, j * cw + (part + 1) * 128)
            out = o_all[j, :, part * 128 : (part + 1) * 128].astype(F32)
            att_out[:, col] = (out * scale_col * att_gain[:, col]).astype(BF16)

    for copy in sends:
        copy.wait_send()

    def drain(j, carry):
        remote(v_all.at[width + j], v_all.at[j], f_ss.at[j], f_rs.at[j], next_plane).wait_send()

        @pl.when(j != w)
        def _():
            remote(
                o_send.at[j], o_all.at[w], o_ss.at[j], o_rs.at[w], {"seq": z * width + j}
            ).wait_send()

        return carry

    lax.fori_loop(0, width, drain, 0)


def local(planes, width, mps, d_model, *args):
    (se_q, se_k, se_v, mr_q, mr_k, att_q, att_k, ids, se_taps, mr_taps, rates, g1, g2, g3) = args
    chans = se_q.shape[1]
    cw = chans // width
    heads = cw // HEAD
    span = width + 1
    vm = pl.BlockSpec(memory_space=pltpu.VMEM)
    anyspec = pl.BlockSpec(memory_space=pl.ANY)
    vmem = pltpu.VMEM
    dma = pltpu.SemaphoreType.DMA
    out = jax.ShapeDtypeStruct((TOK, chans), BF16)
    return pl.pallas_call(
        functools.partial(kernel, planes, width, mps, d_model),
        out_shape=(out, out),
        in_specs=[vm] * 5 + [anyspec] * 2 + [vm] * 7,
        out_specs=(vm, vm),
        scratch_shapes=[
            vmem((2 * TOK, chans), F32),
            vmem((TOK, chans), F32),
            vmem((MR_K, chans), F32),
            vmem((2 * TOK, 128), F32),
            vmem((SE_K, TOK, 128), F32),
            vmem((TOK // 16, TOK + 16, 128), F32),
            vmem((TOK // 16, 24, 8, 128), F32),
            vmem((TOK + 16, 128), F32),
            vmem((32, 128), F32),
            vmem((TOK, 128), F32),
            vmem((16, chans), BF16),
            vmem((16, chans), BF16),
            vmem((TOK, chans), BF16),
            vmem((TOK, chans), BF16),
            vmem((8, 128), F32),
            vmem((8, 128), F32),
            vmem((3, 8, 128), F32),
            vmem((3, mps, 8, 128), F32),
            vmem((8, 128), F32),
            vmem((8, 128), F32),
            vmem((2 * width, 8, 128), F32),
            vmem((2 * width, TOK, cw), BF16),
            vmem((width, TOK, cw), BF16),
            vmem((2 * width, TOK, cw), BF16),
            vmem((span, TOK, TOK), F32),
            vmem((width, heads, TOK, span * TOK), BF16),
            vmem((width, heads, TOK, TOK), F32),
            vmem((width, TOK, cw), BF16),
            vmem((width, TOK, cw), BF16),
            dma((3,)),
            dma((width,)),
            dma((width,)),
            dma((width,)),
            dma((width,)),
            dma((width,)),
            dma((width,)),
            dma((width,)),
            dma((width,)),
            dma((width,)),
            dma((width,)),
            dma((width + 2,)),
            dma((width + 2,)),
            dma((3, mps)),
            dma((3, mps)),
            dma((8,)),
            dma((8,)),
        ],
        compiler_params=pltpu.CompilerParams(
            collective_id=0, has_side_effects=True, vmem_limit_bytes=48 * 1024 * 1024
        ),
    )(
        se_q,
        se_k,
        se_v,
        mr_q,
        mr_k,
        att_q,
        att_k,
        ids.reshape(1, TOK),
        se_taps,
        mr_taps,
        rates.reshape(1, chans),
        g1.reshape(1, chans),
        g2.reshape(1, chans),
        g3.reshape(1, chans),
    )


def solution(mesh, width=8, d_model=D):
    planes = mesh.shape["seq"] // width
    spec = P("seq", "mp")
    return jax.shard_map(
        functools.partial(local, planes, width, mesh.shape["mp"], d_model),
        mesh=mesh,
        in_specs=(spec,) * 7
        + (P("seq"), P(None, "mp"), P(None, "mp"), P("mp"), P("mp"), P("mp"), P("mp")),
        out_specs=(spec, spec),
        check_vma=False,
    )
```

```python
import functools
import math

import jax
import jax.numpy as jnp
import numpy as np
from jax import lax
from jax.experimental import pallas as pl
from jax.experimental.pallas import tpu as pltpu
from jax.sharding import PartitionSpec as P

D = 8192
HEAD = 128
TOK = 128
SE_K = 7
MR_K = 128
MESH = pl.DeviceIdType.MESH
F32 = jnp.float32
BF16 = jnp.bfloat16


def transforms(n):
    k = np.arange(n)[:, None]
    t = np.arange(n)[None, :]
    cos, sin = np.cos(np.pi * k * t / n), np.sin(np.pi * k * t / n)
    sin[0] = np.cos(np.pi * t[0])
    forth = np.concatenate([cos, sin], 0)
    t = t + n
    cos, sin = np.cos(np.pi * k * t / n), np.sin(np.pi * k * t / n)
    sin[0] = np.cos(np.pi * t[0])
    back = np.concatenate([cos, sin], 0) / n
    back[0] /= 2
    back[n] /= 2
    return jnp.asarray(forth, BF16), jnp.asarray(back.T, BF16)


def ring(index, step, size):
    return lax.rem(index + (step + size), size)


def kernel(
    planes,
    width,
    mps,
    d_model,
    se_q_h,
    se_k_h,
    se_v_h,
    mr_q_h,
    mr_k_h,
    att_q,
    att_k,
    ids_h,
    se_taps_h,
    mr_taps_h,
    rates_h,
    se_gain_h,
    mr_gain_h,
    att_gain_h,
    forth_h,
    back_h,
    mr_out,
    att_out,
    se_q,
    se_k,
    se_v,
    mr_q,
    mr_k,
    ids,
    se_taps,
    mr_taps,
    rates,
    se_gain,
    mr_gain,
    att_gain,
    forth,
    back,
    in_sem,
    ue,
    ybuf,
    filt,
    idc,
    m7,
    ma,
    mb,
    um,
    ul,
    sq,
    sh_send,
    sh_recv,
    v_send,
    v_recv,
    r_send,
    r_recv,
    ps_send,
    ps_recv,
    id_send,
    id_prev,
    id_all,
    k_all,
    q_all,
    v_all,
    s_buf,
    p_all,
    linv,
    v_raw,
    v_s,
    hat_a,
    hat_b,
    hat_c,
    hat,
    hat_y,
    u_in,
    m_prior,
    r_col,
    o_acc,
    t_val,
    t_val2,
    t_all,
    r_val,
    r_all,
    o_send,
    o_all,
    loc_sem,
    k_ss,
    k_rs,
    q_ss,
    q_rs,
    v_ss,
    v_rs,
    o_ss,
    o_rs,
    i_ss,
    i_rs,
    f_ss,
    f_rs,
    g_ss,
    g_rs,
    t_ss,
    t_rs,
    ps_ss,
    ps_rs,
    h_ss,
    h_rs,
):
    seq = lax.axis_index("seq")
    mp = lax.axis_index("mp")
    count = planes * width
    z = seq // width
    w = lax.rem(seq, width)
    chans = se_q.shape[1]
    groups = chans // 128
    cw = chans // width
    heads = cw // HEAD
    span = width + 1

    def mate(step):
        return z * width + ring(w, step, width)

    def remote(src, dst, ss, rs, where):
        return pltpu.make_async_remote_copy(
            src_ref=src, dst_ref=dst, send_sem=ss, recv_sem=rs, device_id=where, device_id_type=MESH
        )

    def lanes(g, size=128):
        return pl.ds(pl.multiple_of(g * size, 128), size)

    next_seq = {"seq": ring(seq, 1, count)}
    next_plane = {"seq": ring(seq, width, count)}

    barrier = pltpu.get_barrier_semaphore()
    for step in range(1, width):
        pl.semaphore_signal(barrier, inc=1, device_id={"seq": mate(step)}, device_id_type=MESH)
    for there in range(width):
        pl.semaphore_signal(
            barrier,
            inc=1,
            device_id={"seq": ring(z, -1, planes) * width + there},
            device_id_type=MESH,
        )
    pl.semaphore_signal(barrier, inc=1, device_id={"seq": ring(seq, -1, count)}, device_id_type=MESH)
    for step in range(1, mps):
        pl.semaphore_signal(barrier, inc=1, device_id={"mp": ring(mp, step, mps)}, device_id_type=MESH)

    loads = {}
    for src, dst in (
        (ids_h, ids),
        (se_k_h, se_k),
        (se_v_h, se_v),
        (mr_taps_h, mr_taps),
        (rates_h, rates),
        (forth_h, forth),
        (se_q_h, se_q),
        (mr_k_h, mr_k),
        (se_taps_h, se_taps),
        (se_gain_h, se_gain),
        (mr_q_h, mr_q),
        (mr_gain_h, mr_gain),
        (att_gain_h, att_gain),
        (back_h, back),
    ):
        copy = pltpu.make_async_copy(src, dst, in_sem.at[len(loads)])
        copy.start()
        loads[id(dst)] = copy

    def loaded(*refs):
        for ref in refs:
            loads[id(ref)].wait()

    own_k = pltpu.make_async_copy(att_k.at[:, lanes(w, cw)], k_all.at[width + w], loc_sem.at[0])
    own_q = pltpu.make_async_copy(att_q.at[:, lanes(w, cw)], q_all.at[w], loc_sem.at[1])
    own_k.start()
    own_q.start()

    loaded(ids)
    id_row = ids[...].astype(F32)
    id_send[...] = jnp.broadcast_to(id_row, (8, 128))
    id_all[width + w] = jnp.broadcast_to(id_row, (8, 128))
    idc[TOK:] = jnp.broadcast_to(id_row, (TOK, 128)).T
    loaded(se_k, se_v)
    sh_send[...] = (se_k[TOK - 16 :, :].astype(F32) * se_v[TOK - 16 :, :].astype(F32)).astype(BF16)

    def local_part(g, carry):
        col = lanes(g)
        row = lax.broadcasted_iota(jnp.int32, (MR_K, 128), 0).astype(F32)
        filt[:, col] = mr_taps[:, col].astype(F32) * jnp.exp(-(rates[:, col] * row))
        ue[TOK:, col] = (
            (se_k[:, col].astype(F32) * se_v[:, col].astype(F32)).astype(BF16).astype(F32)
        )
        return carry

    def filter_part(g, carry):
        col = lanes(g, 256)
        full = filt[:, col]
        high = full.astype(BF16)
        low = (full - high.astype(F32)).astype(BF16)
        hat = jnp.dot(forth[...], high, preferred_element_type=F32) + jnp.dot(
            forth[...], low, preferred_element_type=F32
        )
        top = lax.broadcasted_iota(jnp.int32, (TOK, 256), 0) == 0
        hat_a[:, col] = hat[:TOK]
        hat_b[:, col] = jnp.where(top, 0.0, hat[TOK:])
        hat_c[:, col] = jnp.where(top, hat[TOK:], hat[:TOK])
        return carry

    loaded(mr_taps, rates, forth)
    lax.fori_loop(0, groups, local_part, 0)
    lax.fori_loop(0, groups // 2, filter_part, 0)
    idc[:TOK] = jnp.full((TOK, 128), -1.0, F32)
    ue[TOK - 8 : TOK, :] = jnp.zeros((8, chans), F32)
    here = idc[TOK:]
    for tap in range(1, SE_K):
        m7[tap] = (idc[TOK - tap : 2 * TOK - tap] == here).astype(F32)
    sq[...] = jnp.zeros_like(sq)

    def short_rows(start, size, col):
        rows = slice(start, start + size)
        acc = ue[TOK + start : TOK + start + size, col] * se_taps[0:1, col]
        for tap in range(1, SE_K):
            acc += (ue[TOK + start - tap : TOK + start + size - tap, col] * m7[tap, rows, :]) * se_taps[
                tap : tap + 1, col
            ]
        out = se_q[rows, col].astype(F32) * acc
        sq[rows, :] += out * out
        out = out * se_gain[:, col]
        ybuf[rows, col] = out
        v_send[rows, col] = (out * mr_k[rows, col].astype(F32)).astype(BF16)

    def short_part(g, carry):
        for rb in range(TOK // 32):
            short_rows(32 * rb, 32, lanes(g))
        return carry

    blocks = TOK // 16

    def masks(a, carry):
        base = pl.multiple_of(a * 16, 16)
        first = idc[pl.ds(base + TOK, 8), :][0:1, :]
        ma[a] = (idc[TOK:, :] == first).astype(F32)
        ul[...] = idc[pl.ds(base + TOK - 16, 32), :]
        sub = lax.broadcasted_iota(jnp.int32, (8, 128), 0)
        at = 0
        for tile in range(2):
            mine = ul[16 + 8 * tile : 24 + 8 * tile, :]
            for tap in range(8 * tile + 8):
                then = ul[16 + 8 * tile - tap : 24 + 8 * tile - tap, :]
                keep = (mine == then) & (mine != first) & (sub + 8 * tile >= tap)
                mb[a, at] = keep.astype(F32)
                at += 1
        return carry

    lax.fori_loop(0, blocks, masks, 0)
    um[...] = jnp.zeros_like(um)

    loaded(se_q, mr_k, se_taps, se_gain)
    lax.fori_loop(0, groups, short_part, 0)

    pl.semaphore_wait(barrier, (width - 1) + width + 1 + (mps - 1))

    id_next = remote(id_send, id_prev, h_ss.at[0], h_rs.at[0], next_seq)
    id_next.start()
    sh_next = remote(sh_send, sh_recv, h_ss.at[1], h_rs.at[1], next_seq)
    sh_next.start()
    sends = [id_next, sh_next]
    halo = [
        remote(v_send.at[rows], v_recv.at[rows], h_ss.at[at], h_rs.at[at], next_seq)
        for at, rows in ((3, pl.ds(16, TOK - 16)), (4, pl.ds(0, 16)))
    ]
    sends += halo
    for step in range(1, width):
        there = ring(w, step, width)
        copy = remote(
            id_send, id_all.at[width + w], i_ss.at[step], i_rs.at[w], {"seq": mate(step)}
        )
        copy.start()
        sends.append(copy)
        copy = remote(
            att_k.at[:, lanes(there, cw)],
            k_all.at[width + w],
            k_ss.at[step],
            k_rs.at[w],
            {"seq": mate(step)},
        )
        copy.start()
        sends.append(copy)

    halo[0].start()

    id_next.wait_recv()
    idc[:TOK] = jnp.broadcast_to(id_prev[0:1, :], (TOK, 128)).T
    for tap in range(1, SE_K):
        m7[tap, 0:16] = (idc[TOK - tap : TOK + 16 - tap] == idc[TOK : TOK + 16]).astype(F32)
    sh_next.wait_recv()
    ue[TOK - 8 : TOK, :] = sh_recv[...].astype(F32)[8:16, :]
    sq[0:16, :] = jnp.zeros((16, 128), F32)

    def first_rows(g, carry):
        short_rows(0, 16, lanes(g))
        return carry

    lax.fori_loop(0, groups, first_rows, 0)
    halo[1].start()

    def psum_start(which):
        row = jnp.sum(sq[...].T, axis=0, keepdims=True)
        ps_send[which] = jnp.broadcast_to(row, (8, 128))
        copies = []
        for step in range(1, mps):
            copy = remote(
                ps_send.at[which],
                ps_recv.at[which, step],
                ps_ss.at[which, step],
                ps_rs.at[which, step],
                {"mp": ring(mp, step, mps)},
            )
            copy.start()
            copies.append(copy)
        return copies

    def psum_end(which, copies):
        total = ps_send[which]
        for step, copy in enumerate(copies, 1):
            copy.wait_recv()
            total = total + ps_recv[which, step]
        return lax.rsqrt(total / d_model + 1e-06)

    def column(rows8):
        return jnp.broadcast_to(rows8[0:1, :], (TOK, 128)).T

    copies = psum_start(0)
    sends += copies

    m_prior[...] = (idc[:TOK] == idc[TOK : TOK + 1, :]).astype(F32)
    r_own = psum_end(0, copies)
    r_send[...] = r_own
    r_next = remote(r_send, r_recv, h_ss.at[2], h_rs.at[2], next_seq)
    r_next.start()
    sends.append(r_next)
    r_col[...] = column(r_own)

    def medium_part(g, carry):
        col = lanes(g)
        se_out = (ybuf[:, col] * r_col[...]).astype(BF16).astype(F32)
        ue[TOK:, col] = (mr_k[:, col].astype(F32) * se_out).astype(BF16).astype(F32)
        for a in range(blocks):
            size = 16 * a + 16
            base = 16 * a
            win = um.at[a % 2]
            win[8 : 8 + size, :] = ue[TOK : TOK + size, col] * ma[a, 0:size, :]
            acc = [[jnp.zeros((8, 128), F32) for _ in range(4)] for _ in range(2)]
            for phase in range(8):
                wins = [win[8 + 8 * k - phase : 16 + 8 * k - phase, :] for k in range(2 * a + 2)]
                for m in range(2 * a + 2):
                    tap = filt[8 * m + phase : 8 * m + phase + 1, col]
                    for tile in range(2):
                        if 2 * a + tile >= m:
                            acc[tile][phase % 4] += wins[2 * a + tile - m] * tap
            at = 0
            for tile in range(2):
                row = base + 8 * tile
                total = (acc[tile][0] + acc[tile][1]) + (acc[tile][2] + acc[tile][3])
                total = total * ma[a, row : row + 8, :]
                for tap in range(8 * tile + 8):
                    total += (
                        ue[TOK + row - tap : TOK + row + 8 - tap, col] * mb[a, at]
                    ) * filt[tap : tap + 1, col]
                    at += 1
                ybuf[row : row + 8, col] = total
        return carry

    lax.fori_loop(0, groups * 3 // 8, medium_part, 0)

    own_k.wait()
    for step in range(1, width):
        src = ring(w, -step, width)
        remote(
            k_all.at[width + src], k_all.at[width + src], k_ss.at[step], k_rs.at[src], next_seq
        ).wait_recv()
        remote(
            id_all.at[width + src], id_all.at[width + src], i_ss.at[step], i_rs.at[src], next_seq
        ).wait_recv()
    k_next = remote(
        k_all.at[pl.ds(width, width)], k_all.at[pl.ds(0, width)], f_ss.at[width], f_rs.at[width], next_plane
    )
    k_next.start()
    i_next = remote(
        id_all.at[pl.ds(width, width)],
        id_all.at[pl.ds(0, width)],
        f_ss.at[width + 1],
        f_rs.at[width + 1],
        next_plane,
    )
    i_next.start()
    sends += [k_next, i_next]

    lax.fori_loop(groups * 3 // 8, groups, medium_part, 0)

    loaded(mr_q, mr_gain, att_gain, back)
    r_next.wait_recv()
    r_col[...] = column(r_recv[...]) * m_prior[...]
    for copy in halo:
        copy.wait_recv()
    for step in range(1, width):
        there = ring(w, step, width)
        copy = remote(
            att_q.at[:, lanes(there, cw)], q_all.at[w], q_ss.at[step], q_rs.at[w], {"seq": mate(step)}
        )
        copy.start()
        sends.append(copy)
    sq[...] = jnp.zeros_like(sq)

    def prior_part(g, carry):
        wide = lanes(g, 256)
        halves = [lanes(2 * g + half) for half in range(2)]
        factor = r_col[...]
        for half, col in enumerate(halves):
            u_in[:, 128 * half : 128 * half + 128] = (v_recv[:, col].astype(F32) * factor).astype(BF16)
        hat[...] = jnp.dot(forth[...], u_in[...], preferred_element_type=F32)
        hat_y[:TOK, :] = (hat[:TOK] * hat_a[:, wide] - hat[TOK:] * hat_b[:, wide]).astype(BF16)
        hat_y[TOK:, :] = (hat[:TOK] * hat_b[:, wide] + hat[TOK:] * hat_c[:, wide]).astype(BF16)
        prior = jnp.dot(back[...], hat_y[...], preferred_element_type=F32)
        keep = ma[0]
        for half, col in enumerate(halves):
            out = ybuf[:, col] + keep * prior[:, 128 * half : 128 * half + 128]
            out = mr_q[:, col].astype(F32) * out
            ybuf[:, col] = out
            sq[...] += out * out
        return carry

    lax.fori_loop(0, groups // 2, prior_part, 0)

    copies = psum_start(1)
    sends += copies

    def raw_chunk(there):
        for part in range(cw // 128):
            col = lanes(there * (cw // 128) + part)
            v_raw[:, col] = (ybuf[:, col] * mr_gain[:, col]).astype(BF16)

    above = ring(z, 1, planes) * width
    for step in range(width):
        there = ring(w, step, width)
        chunk = v_raw.at[:, lanes(there, cw)]
        raw_chunk(there)
        if step > 0:
            copy = remote(chunk, v_all.at[width + w], v_ss.at[step], v_rs.at[w], {"seq": mate(step)})
            copy.start()
            sends.append(copy)
        copy = remote(chunk, v_all.at[w], f_ss.at[step], f_rs.at[w], {"seq": above + there})
        copy.start()
        sends.append(copy)
    own_v = pltpu.make_async_copy(v_raw.at[:, lanes(w, cw)], v_all.at[width + w], loc_sem.at[2])
    own_v.start()

    r_own = psum_end(1, copies)
    r_val[...] = r_own
    r_all[width + w] = r_own
    for step in range(width):
        there = ring(w, step, width)
        if step > 0:
            copy = remote(
                r_val, r_all.at[width + w], g_ss.at[step], g_rs.at[width + w], {"seq": mate(step)}
            )
            copy.start()
            sends.append(copy)
        copy = remote(
            r_val, r_all.at[w], g_ss.at[width + step], g_rs.at[w], {"seq": above + there}
        )
        copy.start()
        sends.append(copy)
    r_col[...] = column(r_own)

    own_q.wait()
    for step in range(1, width):
        src = ring(w, -step, width)
        remote(q_all.at[src], q_all.at[src], q_ss.at[step], q_rs.at[src], next_seq).wait_recv()
    k_next.wait_recv()
    i_next.wait_recv()

    scale = HEAD**-0.5 * math.log2(math.e)
    tri = lax.broadcasted_iota(jnp.int32, (TOK, TOK), 0) >= lax.broadcasted_iota(
        jnp.int32, (TOK, TOK), 1
    )

    def weights(b):
        id_q = column(id_all[width + b])
        for h in range(heads):
            hl = slice(h * HEAD, (h + 1) * HEAD)
            q = q_all[b, :, hl]
            top = None
            for kk in range(span):
                s = lax.dot_general(
                    q,
                    k_all[b + kk, :, hl],
                    (((1,), (1,)), ((), ())),
                    preferred_element_type=F32,
                )
                keep = id_q == jnp.broadcast_to(id_all[b + kk][0:1, :], (TOK, TOK))
                if kk == span - 1:
                    keep = keep & tri
                s = jnp.where(keep, s * scale, -1e30)
                s_buf[kk] = s
                top = s if top is None else jnp.maximum(top, s)
            top = jnp.max(top, axis=1, keepdims=True)
            total = None
            for kk in range(span):
                e = jnp.exp2(s_buf[kk] - top)
                total = e if total is None else total + e
                p_all[b, h, :, kk * TOK : (kk + 1) * TOK] = e.astype(BF16)
            total = jnp.sum(total, axis=1, keepdims=True)
            linv[b, h] = jnp.broadcast_to(1.0 / total, (TOK, TOK))

    def weigh(i, carry):
        weights(i)
        return carry

    lax.fori_loop(0, width, weigh, 0)

    def norm_out(g, carry):
        col = lanes(g)
        mr_out[:, col] = (ybuf[:, col] * r_col[...] * mr_gain[:, col]).astype(BF16)
        return carry

    lax.fori_loop(0, groups, norm_out, 0)

    def scale_values(slot):
        factor = column(r_all[slot])
        for part in range(cw // 128):
            col = slice(part * 128, (part + 1) * 128)
            v_s[slot, :, col] = (v_all[slot, :, col].astype(F32) * factor).astype(BF16)

    own_v.wait()

    def take_own(i, carry):
        src = ring(w, -i, width)
        slot = width + src

        @pl.when(i != 0)
        def _():
            remote(v_all.at[slot], v_all.at[slot], v_ss.at[0], v_rs.at[src], next_seq).wait_recv()
            remote(r_all.at[slot], r_all.at[slot], g_ss.at[0], g_rs.at[slot], next_seq).wait_recv()

        scale_values(slot)
        return carry

    lax.fori_loop(0, width, take_own, 0)

    for b in range(width):
        for h in range(heads):
            hl = slice(h * HEAD, (h + 1) * HEAD)
            o_acc[b, h] = jnp.dot(
                p_all[b, h, :, (width - b) * TOK :],
                v_s[width : width + b + 1, :, hl].reshape((b + 1) * TOK, HEAD),
                preferred_element_type=F32,
            )

    for b in range(width - 1, -1, -1):
        remote(v_all.at[b], v_all.at[b], v_ss.at[0], f_rs.at[b], next_seq).wait_recv()
        remote(r_all.at[b], r_all.at[b], g_ss.at[0], g_rs.at[b], next_seq).wait_recv()
        scale_values(b)
        squares = None
        for h in range(heads):
            hl = slice(h * HEAD, (h + 1) * HEAD)
            o = o_acc[b, h] + jnp.dot(
                p_all[b, h, :, : (width - b) * TOK],
                v_s[b:width, :, hl].reshape((width - b) * TOK, HEAD),
                preferred_element_type=F32,
            )
            o = o * linv[b, h]
            o_send[b, :, hl] = o.astype(BF16)
            squares = o * o if squares is None else squares + o * o

        @pl.when(w != b)
        def _():
            remote(
                o_send.at[b],
                o_all.at[w],
                o_ss.at[b],
                o_rs.at[w],
                {"seq": z * width + b},
            ).start()

        ps_send[2, b : b + 1, :] = jnp.sum(squares.T, axis=0, keepdims=True)

    copies = []
    for step in range(1, mps):
        copy = remote(
            ps_send.at[2],
            ps_recv.at[2, step],
            ps_ss.at[2, step],
            ps_rs.at[2, step],
            {"mp": ring(mp, step, mps)},
        )
        copy.start()
        copies.append(copy)
    sends += copies
    o_all[w] = o_send[w]
    total = ps_send[2]
    for step, copy in enumerate(copies, 1):
        copy.wait_recv()
        total = total + ps_recv[2, step]
    t_val[...] = total
    t_all[w] = total
    for step in range(1, width):
        copy = remote(t_val, t_all.at[w], t_ss.at[step], t_rs.at[w], {"seq": mate(step)})
        copy.start()
        sends.append(copy)

    def collect(i, total):
        src = ring(w, i, width)

        @pl.when(i != 0)
        def _():
            remote(t_all.at[src], t_all.at[src], t_ss.at[0], t_rs.at[src], next_seq).wait_recv()

        return total + t_all[src]

    t_val2[...] = lax.fori_loop(0, width, collect, jnp.zeros((8, 128), F32))
    mine = t_val2[pl.ds(w, 1), :]
    scale_col = jnp.broadcast_to(lax.rsqrt(mine / d_model + 1e-06), (TOK, 128)).T

    def finish(i, carry):
        src = ring(w, i, width)

        @pl.when(i != 0)
        def _():
            remote(o_all.at[src], o_all.at[src], o_ss.at[src], o_rs.at[src], next_seq).wait_recv()

        for part in range(cw // 128):
            col = lanes(src * (cw // 128) + part)
            out = o_all[src, :, part * 128 : (part + 1) * 128].astype(F32)
            att_out[:, col] = (out * scale_col * att_gain[:, col]).astype(BF16)
        return carry

    lax.fori_loop(0, width, finish, 0)

    for copy in sends:
        copy.wait_send()

    def drain(j, carry):
        @pl.when(j != w)
        def _():
            remote(
                o_send.at[j], o_all.at[w], o_ss.at[j], o_rs.at[w], {"seq": z * width + j}
            ).wait_send()

        return carry

    lax.fori_loop(0, width, drain, 0)


def local(planes, width, mps, d_model, *args):
    (se_q, se_k, se_v, mr_q, mr_k, att_q, att_k, ids, se_taps, mr_taps, rates, g1, g2, g3) = args
    chans = se_q.shape[1]
    cw = chans // width
    heads = cw // HEAD
    span = width + 1
    vm = pl.BlockSpec(memory_space=pltpu.VMEM)
    hbm = pl.BlockSpec(memory_space=pl.ANY)
    vmem = pltpu.VMEM
    dma = pltpu.SemaphoreType.DMA
    out = jax.ShapeDtypeStruct((TOK, chans), BF16)
    return pl.pallas_call(
        functools.partial(kernel, planes, width, mps, d_model),
        out_shape=(out, out),
        in_specs=[hbm] * 16,
        out_specs=(vm, vm),
        scratch_shapes=[
            vmem((TOK, chans), BF16),
            vmem((TOK, chans), BF16),
            vmem((TOK, chans), BF16),
            vmem((TOK, chans), BF16),
            vmem((TOK, chans), BF16),
            vmem((1, TOK), jnp.int32),
            vmem((SE_K, chans), F32),
            vmem((MR_K, chans), BF16),
            vmem((1, chans), F32),
            vmem((1, chans), F32),
            vmem((1, chans), F32),
            vmem((1, chans), F32),
            vmem((2 * TOK, TOK), BF16),
            vmem((TOK, 2 * TOK), BF16),
            dma((14,)),
            vmem((2 * TOK, chans), F32),
            vmem((TOK, chans), F32),
            vmem((MR_K, chans), F32),
            vmem((2 * TOK, 128), F32),
            vmem((SE_K, TOK, 128), F32),
            vmem((TOK // 16, TOK, 128), F32),
            vmem((TOK // 16, 24, 8, 128), F32),
            vmem((2, TOK + 8, 128), F32),
            vmem((32, 128), F32),
            vmem((TOK, 128), F32),
            vmem((16, chans), BF16),
            vmem((16, chans), BF16),
            vmem((TOK, chans), BF16),
            vmem((TOK, chans), BF16),
            vmem((8, 128), F32),
            vmem((8, 128), F32),
            vmem((3, 8, 128), F32),
            vmem((3, mps, 8, 128), F32),
            vmem((8, 128), F32),
            vmem((8, 128), F32),
            vmem((2 * width, 8, 128), F32),
            vmem((2 * width, TOK, cw), BF16),
            vmem((width, TOK, cw), BF16),
            vmem((2 * width, TOK, cw), BF16),
            vmem((span, TOK, TOK), F32),
            vmem((width, heads, TOK, span * TOK), BF16),
            vmem((width, heads, TOK, TOK), F32),
            vmem((TOK, chans), BF16),
            vmem((2 * width, TOK, cw), BF16),
            vmem((TOK, chans), F32),
            vmem((TOK, chans), F32),
            vmem((TOK, chans), F32),
            vmem((2 * TOK, 256), F32),
            vmem((2 * TOK, 256), BF16),
            vmem((TOK, 256), BF16),
            vmem((TOK, 128), F32),
            vmem((TOK, 128), F32),
            vmem((width, heads, TOK, HEAD), F32),
            vmem((8, 128), F32),
            vmem((8, 128), F32),
            vmem((width, 8, 128), F32),
            vmem((8, 128), F32),
            vmem((2 * width, 8, 128), F32),
            vmem((width, TOK, cw), BF16),
            vmem((width, TOK, cw), BF16),
            dma((3,)),
            dma((width,)),
            dma((width,)),
            dma((width,)),
            dma((width,)),
            dma((width,)),
            dma((width,)),
            dma((width,)),
            dma((width,)),
            dma((width,)),
            dma((width,)),
            dma((width + 2,)),
            dma((width + 2,)),
            dma((2 * width,)),
            dma((2 * width,)),
            dma((width,)),
            dma((width,)),
            dma((3, mps)),
            dma((3, mps)),
            dma((8,)),
            dma((8,)),
        ],
        compiler_params=pltpu.CompilerParams(
            collective_id=0, has_side_effects=True, vmem_limit_bytes=60 * 1024 * 1024
        ),
    )(
        se_q,
        se_k,
        se_v,
        mr_q,
        mr_k,
        att_q,
        att_k,
        ids.reshape(1, TOK),
        se_taps,
        mr_taps,
        rates.reshape(1, chans),
        g1.reshape(1, chans),
        g2.reshape(1, chans),
        g3.reshape(1, chans),
        *transforms(TOK),
    )


def solution(mesh, width=8, d_model=D):
    planes = mesh.shape["seq"] // width
    spec = P("seq", "mp")
    return jax.shard_map(
        functools.partial(local, planes, width, mesh.shape["mp"], d_model),
        mesh=mesh,
        in_specs=(spec,) * 7
        + (P("seq"), P(None, "mp"), P(None, "mp"), P("mp"), P("mp"), P("mp"), P("mp")),
        out_specs=(spec, spec),
        check_vma=False,
    )
```

```python
import functools
import math

import jax
import jax.numpy as jnp
import numpy as np
from jax import lax
from jax.experimental import pallas as pl
from jax.experimental.pallas import tpu as pltpu
from jax.sharding import PartitionSpec as P

D = 8192
HEAD = 128
TOK = 128
SE_K = 7
MR_K = 128
MESH = pl.DeviceIdType.MESH
F32 = jnp.float32
BF16 = jnp.bfloat16


def transforms(n):
    k = np.arange(n)[:, None]
    t = np.arange(n)[None, :]
    cos, sin = np.cos(np.pi * k * t / n), np.sin(np.pi * k * t / n)
    sin[0] = np.cos(np.pi * t[0])
    forth = np.concatenate([cos, sin], 0)
    t = t + n
    cos, sin = np.cos(np.pi * k * t / n), np.sin(np.pi * k * t / n)
    sin[0] = np.cos(np.pi * t[0])
    back = np.concatenate([cos, sin], 0) / n
    back[0] /= 2
    back[n] /= 2
    return jnp.asarray(forth, BF16), jnp.asarray(back.T, BF16)


def ring(index, step, size):
    return lax.rem(index + (step + size), size)


def kernel(
    planes,
    width,
    mps,
    d_model,
    se_q_h,
    se_k_h,
    se_v_h,
    mr_q_h,
    mr_k_h,
    att_q,
    att_k,
    ids_h,
    se_taps_h,
    mr_taps_h,
    rates_h,
    se_gain_h,
    mr_gain_h,
    att_gain_h,
    forth_h,
    back_h,
    mr_out,
    att_out,
    se_q,
    se_k,
    se_v,
    mr_q,
    mr_k,
    ids,
    se_taps,
    mr_taps,
    rates,
    se_gain,
    mr_gain,
    att_gain,
    forth,
    back,
    in_sem,
    ue,
    ybuf,
    filt,
    idc,
    m7,
    ma,
    mb,
    um,
    ul,
    sq,
    sh_send,
    sh_recv,
    v_send,
    v_recv,
    r_send,
    r_recv,
    ps_send,
    ps_recv,
    id_send,
    id_prev,
    id_all,
    k_all,
    q_all,
    v_all,
    s_buf,
    p_all,
    linv,
    v_raw,
    v_s,
    hat_a,
    hat_b,
    hat_c,
    hat,
    hat_y,
    u_in,
    m_prior,
    r_col,
    o_acc,
    t_val,
    t_val2,
    t_all,
    r_val,
    r_all,
    o_send,
    o_all,
    loc_sem,
    k_ss,
    k_rs,
    q_ss,
    q_rs,
    v_ss,
    v_rs,
    o_ss,
    o_rs,
    i_ss,
    i_rs,
    f_ss,
    f_rs,
    g_ss,
    g_rs,
    kf_ss,
    kf_rs,
    if_ss,
    if_rs,
    gf_ss,
    gf_rs,
    t_ss,
    t_rs,
    ps_ss,
    ps_rs,
    h_ss,
    h_rs,
):
    seq = lax.axis_index("seq")
    mp = lax.axis_index("mp")
    count = planes * width
    z = seq // width
    w = lax.rem(seq, width)
    chans = se_q.shape[1]
    groups = chans // 128
    cw = chans // width
    heads = cw // HEAD
    span = width + 1

    def mate(step):
        return z * width + ring(w, step, width)

    def remote(src, dst, ss, rs, where):
        return pltpu.make_async_remote_copy(
            src_ref=src, dst_ref=dst, send_sem=ss, recv_sem=rs, device_id=where, device_id_type=MESH
        )

    def lanes(g, size=128):
        return pl.ds(pl.multiple_of(g * size, 128), size)

    next_seq = {"seq": ring(seq, 1, count)}
    next_plane = {"seq": ring(seq, width, count)}

    barrier = pltpu.get_barrier_semaphore()
    for step in range(1, width):
        pl.semaphore_signal(barrier, inc=1, device_id={"seq": mate(step)}, device_id_type=MESH)
    pl.semaphore_signal(barrier, inc=1, device_id={"seq": ring(seq, -width, count)}, device_id_type=MESH)
    pl.semaphore_signal(barrier, inc=1, device_id={"seq": ring(seq, -1, count)}, device_id_type=MESH)
    for step in range(1, mps):
        pl.semaphore_signal(barrier, inc=1, device_id={"mp": ring(mp, step, mps)}, device_id_type=MESH)

    loads = {}
    for src, dst in (
        (ids_h, ids),
        (se_k_h, se_k),
        (se_v_h, se_v),
        (mr_taps_h, mr_taps),
        (rates_h, rates),
        (forth_h, forth),
        (se_q_h, se_q),
        (mr_k_h, mr_k),
        (se_taps_h, se_taps),
        (se_gain_h, se_gain),
        (mr_q_h, mr_q),
        (mr_gain_h, mr_gain),
        (att_gain_h, att_gain),
        (back_h, back),
    ):
        copy = pltpu.make_async_copy(src, dst, in_sem.at[len(loads)])
        copy.start()
        loads[id(dst)] = copy

    def loaded(*refs):
        for ref in refs:
            loads[id(ref)].wait()

    @pl.when(z == 0)
    def _():
        def clear(j, carry):
            k_all[j] = jnp.zeros((TOK, cw), BF16)
            v_all[j] = jnp.zeros((TOK, cw), BF16)
            r_all[j] = jnp.zeros((8, 128), F32)
            id_all[j] = jnp.full((8, 128), -1.0, F32)
            return carry

        lax.fori_loop(0, width, clear, 0)

    own_k = pltpu.make_async_copy(att_k.at[:, lanes(w, cw)], k_all.at[width + w], loc_sem.at[0])
    own_q = pltpu.make_async_copy(att_q.at[:, lanes(w, cw)], q_all.at[w], loc_sem.at[1])
    own_k.start()
    own_q.start()

    loaded(ids)
    id_row = ids[...].astype(F32)
    id_send[...] = jnp.broadcast_to(id_row, (8, 128))
    id_all[width + w] = jnp.broadcast_to(id_row, (8, 128))
    idc[TOK:] = jnp.broadcast_to(id_row, (TOK, 128)).T
    loaded(se_k, se_v)
    sh_send[...] = (se_k[TOK - 16 :, :].astype(F32) * se_v[TOK - 16 :, :].astype(F32)).astype(BF16)

    def local_part(g, carry):
        col = lanes(g)
        row = lax.broadcasted_iota(jnp.int32, (MR_K, 128), 0).astype(F32)
        filt[:, col] = mr_taps[:, col].astype(F32) * jnp.exp(-(rates[:, col] * row))
        ue[TOK:, col] = (
            (se_k[:, col].astype(F32) * se_v[:, col].astype(F32)).astype(BF16).astype(F32)
        )
        return carry

    def filter_part(g, carry):
        col = lanes(g, 256)
        full = filt[:, col]
        high = full.astype(BF16)
        low = (full - high.astype(F32)).astype(BF16)
        hat = jnp.dot(forth[...], high, preferred_element_type=F32) + jnp.dot(
            forth[...], low, preferred_element_type=F32
        )
        top = lax.broadcasted_iota(jnp.int32, (TOK, 256), 0) == 0
        hat_a[:, col] = hat[:TOK]
        hat_b[:, col] = jnp.where(top, 0.0, hat[TOK:])
        hat_c[:, col] = jnp.where(top, hat[TOK:], hat[:TOK])
        return carry

    loaded(mr_taps, rates, forth)
    lax.fori_loop(0, groups, local_part, 0)
    lax.fori_loop(0, groups // 2, filter_part, 0)
    idc[:TOK] = jnp.full((TOK, 128), -1.0, F32)
    ue[TOK - 8 : TOK, :] = jnp.zeros((8, chans), F32)
    here = idc[TOK:]
    for tap in range(1, SE_K):
        m7[tap] = (idc[TOK - tap : 2 * TOK - tap] == here).astype(F32)
    sq[...] = jnp.zeros_like(sq)

    def short_rows(start, size, col):
        rows = slice(start, start + size)
        acc = ue[TOK + start : TOK + start + size, col] * se_taps[0:1, col]
        for tap in range(1, SE_K):
            acc += (ue[TOK + start - tap : TOK + start + size - tap, col] * m7[tap, rows, :]) * se_taps[
                tap : tap + 1, col
            ]
        out = se_q[rows, col].astype(F32) * acc
        sq[rows, :] += out * out
        out = out * se_gain[:, col]
        ybuf[rows, col] = out
        v_send[rows, col] = (out * mr_k[rows, col].astype(F32)).astype(BF16)

    def short_part(g, carry):
        for rb in range(TOK // 32):
            short_rows(32 * rb, 32, lanes(g))
        return carry

    blocks = TOK // 16

    def masks(a, carry):
        base = pl.multiple_of(a * 16, 16)
        first = idc[pl.ds(base + TOK, 8), :][0:1, :]
        ma[a] = (idc[TOK:, :] == first).astype(F32)
        ul[...] = idc[pl.ds(base + TOK - 16, 32), :]
        sub = lax.broadcasted_iota(jnp.int32, (8, 128), 0)
        at = 0
        for tile in range(2):
            mine = ul[16 + 8 * tile : 24 + 8 * tile, :]
            for tap in range(8 * tile + 8):
                then = ul[16 + 8 * tile - tap : 24 + 8 * tile - tap, :]
                keep = (mine == then) & (mine != first) & (sub + 8 * tile >= tap)
                mb[a, at] = keep.astype(F32)
                at += 1
        return carry

    lax.fori_loop(0, blocks, masks, 0)
    um[...] = jnp.zeros_like(um)

    loaded(se_q, mr_k, se_taps, se_gain)
    lax.fori_loop(0, groups, short_part, 0)

    pl.semaphore_wait(barrier, (width - 1) + 2 + (mps - 1))

    id_next = remote(id_send, id_prev, h_ss.at[0], h_rs.at[0], next_seq)
    id_next.start()
    sh_next = remote(sh_send, sh_recv, h_ss.at[1], h_rs.at[1], next_seq)
    sh_next.start()
    sends = [id_next, sh_next]
    halo = [
        remote(v_send.at[rows], v_recv.at[rows], h_ss.at[at], h_rs.at[at], next_seq)
        for at, rows in ((3, pl.ds(16, TOK - 16)), (4, pl.ds(0, 16)))
    ]
    sends += halo
    halo[0].start()
    for step in range(1, width):
        there = ring(w, step, width)
        copy = remote(
            id_send, id_all.at[width + w], i_ss.at[step], i_rs.at[w], {"seq": mate(step)}
        )
        copy.start()
        sends.append(copy)
        copy = remote(
            att_k.at[:, lanes(there, cw)],
            k_all.at[width + w],
            k_ss.at[step],
            k_rs.at[w],
            {"seq": mate(step)},
        )
        copy.start()
        sends.append(copy)

    id_next.wait_recv()
    idc[:TOK] = jnp.broadcast_to(id_prev[0:1, :], (TOK, 128)).T
    for tap in range(1, SE_K):
        m7[tap, 0:16] = (idc[TOK - tap : TOK + 16 - tap] == idc[TOK : TOK + 16]).astype(F32)
    sh_next.wait_recv()
    ue[TOK - 8 : TOK, :] = sh_recv[...].astype(F32)[8:16, :]
    sq[0:16, :] = jnp.zeros((16, 128), F32)

    def first_rows(g, carry):
        short_rows(0, 16, lanes(g))
        return carry

    lax.fori_loop(0, groups, first_rows, 0)
    halo[1].start()

    def psum_start(which):
        row = jnp.sum(sq[...].T, axis=0, keepdims=True)
        ps_send[which] = jnp.broadcast_to(row, (8, 128))
        copies = []
        for step in range(1, mps):
            copy = remote(
                ps_send.at[which],
                ps_recv.at[which, step],
                ps_ss.at[which, step],
                ps_rs.at[which, step],
                {"mp": ring(mp, step, mps)},
            )
            copy.start()
            copies.append(copy)
        return copies

    def psum_end(which, copies):
        total = ps_send[which]
        for step, copy in enumerate(copies, 1):
            copy.wait_recv()
            total = total + ps_recv[which, step]
        return lax.rsqrt(total / d_model + 1e-06)

    def column(rows8):
        return jnp.broadcast_to(rows8[0:1, :], (TOK, 128)).T

    copies = psum_start(0)
    sends += copies

    m_prior[...] = (idc[:TOK] == idc[TOK : TOK + 1, :]).astype(F32)
    r_own = psum_end(0, copies)
    r_send[...] = r_own
    r_next = remote(r_send, r_recv, h_ss.at[2], h_rs.at[2], next_seq)
    r_next.start()
    sends.append(r_next)
    r_col[...] = column(r_own)

    def medium_part(g, carry):
        col = lanes(g)
        se_out = (ybuf[:, col] * r_col[...]).astype(BF16).astype(F32)
        ue[TOK:, col] = (mr_k[:, col].astype(F32) * se_out).astype(BF16).astype(F32)
        for a in range(blocks):
            size = 16 * a + 16
            base = 16 * a
            win = um.at[a % 2]
            win[8 : 8 + size, :] = ue[TOK : TOK + size, col] * ma[a, 0:size, :]
            acc = [[jnp.zeros((8, 128), F32) for _ in range(4)] for _ in range(2)]
            for phase in range(8):
                wins = [win[8 + 8 * k - phase : 16 + 8 * k - phase, :] for k in range(2 * a + 2)]
                for m in range(2 * a + 2):
                    tap = filt[8 * m + phase : 8 * m + phase + 1, col]
                    for tile in range(2):
                        if 2 * a + tile >= m:
                            acc[tile][phase % 4] += wins[2 * a + tile - m] * tap
            at = 0
            for tile in range(2):
                row = base + 8 * tile
                total = (acc[tile][0] + acc[tile][1]) + (acc[tile][2] + acc[tile][3])
                total = total * ma[a, row : row + 8, :]
                for tap in range(8 * tile + 8):
                    total += (
                        ue[TOK + row - tap : TOK + row + 8 - tap, col] * mb[a, at]
                    ) * filt[tap : tap + 1, col]
                    at += 1
                ybuf[row : row + 8, col] = total
        return carry

    def relay_key(src):
        return (
            remote(k_all.at[width + src], k_all.at[src], kf_ss.at[src], kf_rs.at[src], next_plane),
            remote(id_all.at[width + src], id_all.at[src], if_ss.at[src], if_rs.at[src], next_plane),
        )

    def medium_and_relay(g, carry):
        medium_part(g, carry)
        i = g - relay_from
        src = ring(w, -i, width)

        @pl.when(i != 0)
        def _():
            slot = width + src
            remote(k_all.at[slot], k_all.at[slot], k_ss.at[0], k_rs.at[src], next_seq).wait_recv()
            remote(id_all.at[slot], id_all.at[slot], i_ss.at[0], i_rs.at[src], next_seq).wait_recv()

        @pl.when(z < planes - 1)
        def _():
            for copy in relay_key(src):
                copy.start()

        return carry

    relay_from = groups - width
    lax.fori_loop(0, relay_from, medium_part, 0)
    own_k.wait()
    lax.fori_loop(relay_from, groups, medium_and_relay, 0)

    loaded(mr_q, mr_gain, att_gain, back)
    r_next.wait_recv()
    r_col[...] = column(r_recv[...]) * m_prior[...]
    for copy in halo:
        copy.wait_recv()
    for step in range(1, width):
        there = ring(w, step, width)
        copy = remote(
            att_q.at[:, lanes(there, cw)], q_all.at[w], q_ss.at[step], q_rs.at[w], {"seq": mate(step)}
        )
        copy.start()
        sends.append(copy)
    sq[...] = jnp.zeros_like(sq)

    def prior_part(g, carry):
        wide = lanes(g, 256)
        halves = [lanes(2 * g + half) for half in range(2)]
        factor = r_col[...]
        for half, col in enumerate(halves):
            u_in[:, 128 * half : 128 * half + 128] = (v_recv[:, col].astype(F32) * factor).astype(BF16)
        hat[...] = jnp.dot(forth[...], u_in[...], preferred_element_type=F32)
        hat_y[:TOK, :] = (hat[:TOK] * hat_a[:, wide] - hat[TOK:] * hat_b[:, wide]).astype(BF16)
        hat_y[TOK:, :] = (hat[:TOK] * hat_b[:, wide] + hat[TOK:] * hat_c[:, wide]).astype(BF16)
        prior = jnp.dot(back[...], hat_y[...], preferred_element_type=F32)
        keep = ma[0]
        for half, col in enumerate(halves):
            out = ybuf[:, col] + keep * prior[:, 128 * half : 128 * half + 128]
            out = mr_q[:, col].astype(F32) * out
            ybuf[:, col] = out
            sq[...] += out * out
        return carry

    lax.fori_loop(0, groups // 2, prior_part, 0)

    copies = psum_start(1)
    sends += copies

    def raw_chunk(there):
        for part in range(cw // 128):
            col = lanes(there * (cw // 128) + part)
            v_raw[:, col] = (ybuf[:, col] * mr_gain[:, col]).astype(BF16)

    for step in range(1, width):
        there = ring(w, step, width)
        raw_chunk(there)
        copy = remote(
            v_raw.at[:, lanes(there, cw)], v_all.at[width + w], v_ss.at[step], v_rs.at[w], {"seq": mate(step)}
        )
        copy.start()
        sends.append(copy)
    raw_chunk(w)
    own_v = pltpu.make_async_copy(v_raw.at[:, lanes(w, cw)], v_all.at[width + w], loc_sem.at[2])
    own_v.start()

    r_own = psum_end(1, copies)
    r_val[...] = r_own
    r_all[width + w] = r_own
    for step in range(1, width):
        copy = remote(r_val, r_all.at[width + w], g_ss.at[step], g_rs.at[w], {"seq": mate(step)})
        copy.start()
        sends.append(copy)
    r_col[...] = column(r_own)

    own_q.wait()
    for step in range(1, width):
        src = ring(w, -step, width)
        remote(q_all.at[src], q_all.at[src], q_ss.at[step], q_rs.at[src], next_seq).wait_recv()

    def take_keys(src, carry):
        @pl.when(z > 0)
        def _():
            for copy in relay_key(src):
                copy.wait_recv()

        return carry

    lax.fori_loop(0, width, take_keys, 0)

    scale = HEAD**-0.5 * math.log2(math.e)
    tri = lax.broadcasted_iota(jnp.int32, (TOK, TOK), 0) >= lax.broadcasted_iota(
        jnp.int32, (TOK, TOK), 1
    )

    def weights(b):
        id_q = column(id_all[width + b])
        for h in range(heads):
            hl = slice(h * HEAD, (h + 1) * HEAD)
            q = q_all[b, :, hl]
            top = None
            for kk in range(span):
                s = lax.dot_general(
                    q,
                    k_all[b + kk, :, hl],
                    (((1,), (1,)), ((), ())),
                    preferred_element_type=F32,
                )
                keep = id_q == jnp.broadcast_to(id_all[b + kk][0:1, :], (TOK, TOK))
                if kk == span - 1:
                    keep = keep & tri
                s = jnp.where(keep, s * scale, -1e30)
                s_buf[kk] = s
                top = s if top is None else jnp.maximum(top, s)
            top = jnp.max(top, axis=1, keepdims=True)
            total = None
            for kk in range(span):
                e = jnp.exp2(s_buf[kk] - top)
                total = e if total is None else total + e
                p_all[b, h, :, kk * TOK : (kk + 1) * TOK] = e.astype(BF16)
            total = jnp.sum(total, axis=1, keepdims=True)
            linv[b, h] = jnp.broadcast_to(1.0 / total, (TOK, TOK))

    own_v.wait()

    def relay_value(src):
        return remote(v_all.at[width + src], v_all.at[src], f_ss.at[src], f_rs.at[src], next_plane)

    def relay_factor(src):
        return remote(r_all.at[width + src], r_all.at[src], gf_ss.at[src], gf_rs.at[src], next_plane)

    def weigh(i, carry):
        src = ring(w, -i, width)
        slot = width + src

        @pl.when(i != 0)
        def _():
            remote(v_all.at[slot], v_all.at[slot], v_ss.at[0], v_rs.at[src], next_seq).wait_recv()

        @pl.when(z < planes - 1)
        def _():
            relay_value(src).start()

        weights(i)
        return carry

    lax.fori_loop(0, width, weigh, 0)

    def norm_out(g, carry):
        col = lanes(g)
        mr_out[:, col] = (ybuf[:, col] * r_col[...] * mr_gain[:, col]).astype(BF16)
        return carry

    lax.fori_loop(0, groups, norm_out, 0)

    def scale_values(slot):
        factor = column(r_all[slot])
        for part in range(cw // 128):
            col = slice(part * 128, (part + 1) * 128)
            v_s[slot, :, col] = (v_all[slot, :, col].astype(F32) * factor).astype(BF16)

    def take_own(i, carry):
        src = ring(w, -i, width)
        slot = width + src

        @pl.when(i != 0)
        def _():
            remote(r_all.at[slot], r_all.at[slot], g_ss.at[0], g_rs.at[src], next_seq).wait_recv()

        @pl.when(z < planes - 1)
        def _():
            relay_factor(src).start()

        scale_values(slot)
        return carry

    lax.fori_loop(0, width, take_own, 0)

    for b in range(width):
        for h in range(heads):
            hl = slice(h * HEAD, (h + 1) * HEAD)
            o_acc[b, h] = jnp.dot(
                p_all[b, h, :, (width - b) * TOK :],
                v_s[width : width + b + 1, :, hl].reshape((b + 1) * TOK, HEAD),
                preferred_element_type=F32,
            )

    for b in range(width - 1, -1, -1):
        @pl.when(z > 0)
        def _():
            relay_value(b).wait_recv()
            relay_factor(b).wait_recv()

        scale_values(b)
        squares = None
        for h in range(heads):
            hl = slice(h * HEAD, (h + 1) * HEAD)
            o = o_acc[b, h] + jnp.dot(
                p_all[b, h, :, : (width - b) * TOK],
                v_s[b:width, :, hl].reshape((width - b) * TOK, HEAD),
                preferred_element_type=F32,
            )
            o = o * linv[b, h]
            o_send[b, :, hl] = o.astype(BF16)
            squares = o * o if squares is None else squares + o * o

        @pl.when(w != b)
        def _():
            remote(
                o_send.at[b],
                o_all.at[w],
                o_ss.at[b],
                o_rs.at[w],
                {"seq": z * width + b},
            ).start()

        ps_send[2, b : b + 1, :] = jnp.sum(squares.T, axis=0, keepdims=True)

    copies = []
    for step in range(1, mps):
        copy = remote(
            ps_send.at[2],
            ps_recv.at[2, step],
            ps_ss.at[2, step],
            ps_rs.at[2, step],
            {"mp": ring(mp, step, mps)},
        )
        copy.start()
        copies.append(copy)
    sends += copies
    o_all[w] = o_send[w]
    total = ps_send[2]
    for step, copy in enumerate(copies, 1):
        copy.wait_recv()
        total = total + ps_recv[2, step]
    t_val[...] = total
    t_all[w] = total
    for step in range(1, width):
        copy = remote(t_val, t_all.at[w], t_ss.at[step], t_rs.at[w], {"seq": mate(step)})
        copy.start()
        sends.append(copy)

    def collect(i, total):
        src = ring(w, i, width)

        @pl.when(i != 0)
        def _():
            remote(t_all.at[src], t_all.at[src], t_ss.at[0], t_rs.at[src], next_seq).wait_recv()

        return total + t_all[src]

    t_val2[...] = lax.fori_loop(0, width, collect, jnp.zeros((8, 128), F32))
    mine = t_val2[pl.ds(w, 1), :]
    scale_col = jnp.broadcast_to(lax.rsqrt(mine / d_model + 1e-06), (TOK, 128)).T

    def finish(i, carry):
        src = ring(w, i, width)

        @pl.when(i != 0)
        def _():
            remote(o_all.at[src], o_all.at[src], o_ss.at[src], o_rs.at[src], next_seq).wait_recv()

        for part in range(cw // 128):
            col = lanes(src * (cw // 128) + part)
            out = o_all[src, :, part * 128 : (part + 1) * 128].astype(F32)
            att_out[:, col] = (out * scale_col * att_gain[:, col]).astype(BF16)
        return carry

    lax.fori_loop(0, width, finish, 0)

    for copy in sends:
        copy.wait_send()

    def drain(j, carry):
        @pl.when(z < planes - 1)
        def _():
            for copy in (*relay_key(j), relay_value(j), relay_factor(j)):
                copy.wait_send()
        @pl.when(j != w)
        def _():
            remote(
                o_send.at[j], o_all.at[w], o_ss.at[j], o_rs.at[w], {"seq": z * width + j}
            ).wait_send()

        return carry

    lax.fori_loop(0, width, drain, 0)


def local(planes, width, mps, d_model, *args):
    (se_q, se_k, se_v, mr_q, mr_k, att_q, att_k, ids, se_taps, mr_taps, rates, g1, g2, g3) = args
    chans = se_q.shape[1]
    cw = chans // width
    heads = cw // HEAD
    span = width + 1
    vm = pl.BlockSpec(memory_space=pltpu.VMEM)
    hbm = pl.BlockSpec(memory_space=pl.ANY)
    vmem = pltpu.VMEM
    dma = pltpu.SemaphoreType.DMA
    out = jax.ShapeDtypeStruct((TOK, chans), BF16)
    return pl.pallas_call(
        functools.partial(kernel, planes, width, mps, d_model),
        out_shape=(out, out),
        in_specs=[hbm] * 16,
        out_specs=(vm, vm),
        scratch_shapes=[
            vmem((TOK, chans), BF16),
            vmem((TOK, chans), BF16),
            vmem((TOK, chans), BF16),
            vmem((TOK, chans), BF16),
            vmem((TOK, chans), BF16),
            vmem((1, TOK), jnp.int32),
            vmem((SE_K, chans), F32),
            vmem((MR_K, chans), BF16),
            vmem((1, chans), F32),
            vmem((1, chans), F32),
            vmem((1, chans), F32),
            vmem((1, chans), F32),
            vmem((2 * TOK, TOK), BF16),
            vmem((TOK, 2 * TOK), BF16),
            dma((14,)),
            vmem((2 * TOK, chans), F32),
            vmem((TOK, chans), F32),
            vmem((MR_K, chans), F32),
            vmem((2 * TOK, 128), F32),
            vmem((SE_K, TOK, 128), F32),
            vmem((TOK // 16, TOK, 128), F32),
            vmem((TOK // 16, 24, 8, 128), F32),
            vmem((2, TOK + 8, 128), F32),
            vmem((32, 128), F32),
            vmem((TOK, 128), F32),
            vmem((16, chans), BF16),
            vmem((16, chans), BF16),
            vmem((TOK, chans), BF16),
            vmem((TOK, chans), BF16),
            vmem((8, 128), F32),
            vmem((8, 128), F32),
            vmem((3, 8, 128), F32),
            vmem((3, mps, 8, 128), F32),
            vmem((8, 128), F32),
            vmem((8, 128), F32),
            vmem((2 * width, 8, 128), F32),
            vmem((2 * width, TOK, cw), BF16),
            vmem((width, TOK, cw), BF16),
            vmem((2 * width, TOK, cw), BF16),
            vmem((span, TOK, TOK), F32),
            vmem((width, heads, TOK, span * TOK), BF16),
            vmem((width, heads, TOK, TOK), F32),
            vmem((TOK, chans), BF16),
            vmem((2 * width, TOK, cw), BF16),
            vmem((TOK, chans), F32),
            vmem((TOK, chans), F32),
            vmem((TOK, chans), F32),
            vmem((2 * TOK, 256), F32),
            vmem((2 * TOK, 256), BF16),
            vmem((TOK, 256), BF16),
            vmem((TOK, 128), F32),
            vmem((TOK, 128), F32),
            vmem((width, heads, TOK, HEAD), F32),
            vmem((8, 128), F32),
            vmem((8, 128), F32),
            vmem((width, 8, 128), F32),
            vmem((8, 128), F32),
            vmem((2 * width, 8, 128), F32),
            vmem((width, TOK, cw), BF16),
            vmem((width, TOK, cw), BF16),
            dma((3,)),
            dma((width,)),
            dma((width,)),
            dma((width,)),
            dma((width,)),
            dma((width,)),
            dma((width,)),
            dma((width,)),
            dma((width,)),
            dma((width,)),
            dma((width,)),
            dma((width,)),
            dma((width,)),
            dma((width,)),
            dma((width,)),
            dma((width,)),
            dma((width,)),
            dma((width,)),
            dma((width,)),
            dma((width,)),
            dma((width,)),
            dma((width,)),
            dma((width,)),
            dma((3, mps)),
            dma((3, mps)),
            dma((8,)),
            dma((8,)),
        ],
        compiler_params=pltpu.CompilerParams(
            collective_id=0, has_side_effects=True, vmem_limit_bytes=60 * 1024 * 1024
        ),
    )(
        se_q,
        se_k,
        se_v,
        mr_q,
        mr_k,
        att_q,
        att_k,
        ids.reshape(1, TOK),
        se_taps,
        mr_taps,
        rates.reshape(1, chans),
        g1.reshape(1, chans),
        g2.reshape(1, chans),
        g3.reshape(1, chans),
        *transforms(TOK),
    )


def solution(mesh, width=8, d_model=D):
    planes = mesh.shape["seq"] // width
    spec = P("seq", "mp")
    return jax.shard_map(
        functools.partial(local, planes, width, mesh.shape["mp"], d_model),
        mesh=mesh,
        in_specs=(spec,) * 7
        + (P("seq"), P(None, "mp"), P(None, "mp"), P("mp"), P("mp"), P("mp"), P("mp")),
        out_specs=(spec, spec),
        check_vma=False,
    )
```

```python
import functools
import math

import jax
import jax.numpy as jnp
import numpy as np
from jax import lax
from jax.experimental import pallas as pl
from jax.experimental.pallas import tpu as pltpu
from jax.sharding import PartitionSpec as P

D = 8192
HEAD = 128
TOK = 128
SE_K = 7
MR_K = 128
MESH = pl.DeviceIdType.MESH
F32 = jnp.float32
BF16 = jnp.bfloat16


def transforms(n):
    k = np.arange(n)[:, None]
    t = np.arange(n)[None, :]
    cos, sin = np.cos(np.pi * k * t / n), np.sin(np.pi * k * t / n)
    sin[0] = np.cos(np.pi * t[0])
    forth = np.concatenate([cos, sin], 0)
    t = t + n
    cos, sin = np.cos(np.pi * k * t / n), np.sin(np.pi * k * t / n)
    sin[0] = np.cos(np.pi * t[0])
    back = np.concatenate([cos, sin], 0) / n
    back[0] /= 2
    back[n] /= 2
    return jnp.asarray(forth, BF16), jnp.asarray(back.T, BF16)


def ring(index, step, size):
    return lax.rem(index + (step + size), size)


def kernel(
    planes,
    width,
    mps,
    d_model,
    se_q_h,
    se_k_h,
    se_v_h,
    mr_q_h,
    mr_k_h,
    att_q,
    att_k,
    ids_h,
    se_taps_h,
    mr_taps_h,
    rates_h,
    se_gain_h,
    mr_gain_h,
    att_gain_h,
    forth_h,
    back_h,
    mr_out,
    att_out,
    se_q,
    se_k,
    se_v,
    mr_q,
    mr_k,
    ids,
    se_taps,
    mr_taps,
    rates,
    se_gain,
    mr_gain,
    att_gain,
    forth,
    back,
    in_sem,
    ue,
    ybuf,
    filt,
    idc,
    m7,
    ma,
    mb,
    um,
    ul,
    sq,
    sh_send,
    sh_recv,
    v_send,
    v_recv,
    r_send,
    r_recv,
    ps_send,
    ps_recv,
    id_send,
    id_prev,
    id_all,
    k_all,
    q_all,
    v_all,
    s_buf,
    p_all,
    linv,
    v_raw,
    v_s,
    hat_a,
    hat_b,
    hat_c,
    hat,
    hat_y,
    u_in,
    m_prior,
    r_col,
    o_acc,
    t_val,
    t_val2,
    t_all,
    r_val,
    r_all,
    o_send,
    o_all,
    loc_sem,
    k_ss,
    k_rs,
    q_ss,
    q_rs,
    v_ss,
    v_rs,
    o_ss,
    o_rs,
    i_ss,
    i_rs,
    f_ss,
    f_rs,
    g_ss,
    g_rs,
    kf_ss,
    kf_rs,
    if_ss,
    if_rs,
    gf_ss,
    gf_rs,
    t_ss,
    t_rs,
    ps_ss,
    ps_rs,
    h_ss,
    h_rs,
):
    seq = lax.axis_index("seq")
    mp = lax.axis_index("mp")
    count = planes * width
    z = seq // width
    w = lax.rem(seq, width)
    chans = se_q.shape[1]
    groups = chans // 128
    cw = chans // width
    heads = cw // HEAD
    span = width + 1

    def mate(step):
        return z * width + ring(w, step, width)

    def remote(src, dst, ss, rs, where):
        return pltpu.make_async_remote_copy(
            src_ref=src, dst_ref=dst, send_sem=ss, recv_sem=rs, device_id=where, device_id_type=MESH
        )

    def lanes(g, size=128):
        return pl.ds(pl.multiple_of(g * size, 128), size)

    next_seq = {"seq": ring(seq, 1, count)}
    next_plane = {"seq": ring(seq, width, count)}

    barrier = pltpu.get_barrier_semaphore()
    for step in range(1, width):
        pl.semaphore_signal(barrier, inc=1, device_id={"seq": mate(step)}, device_id_type=MESH)
    pl.semaphore_signal(barrier, inc=1, device_id={"seq": ring(seq, -width, count)}, device_id_type=MESH)
    pl.semaphore_signal(barrier, inc=1, device_id={"seq": ring(seq, -1, count)}, device_id_type=MESH)
    for step in range(1, mps):
        pl.semaphore_signal(barrier, inc=1, device_id={"mp": ring(mp, step, mps)}, device_id_type=MESH)

    loads = {}
    for src, dst in (
        (ids_h, ids),
        (se_k_h, se_k),
        (se_v_h, se_v),
        (mr_taps_h, mr_taps),
        (rates_h, rates),
        (forth_h, forth),
        (se_q_h, se_q),
        (mr_k_h, mr_k),
        (se_taps_h, se_taps),
        (se_gain_h, se_gain),
        (mr_q_h, mr_q),
        (mr_gain_h, mr_gain),
        (att_gain_h, att_gain),
        (back_h, back),
    ):
        copy = pltpu.make_async_copy(src, dst, in_sem.at[len(loads)])
        copy.start()
        loads[id(dst)] = copy

    def loaded(*refs):
        for ref in refs:
            loads[id(ref)].wait()

    @pl.when(z == 0)
    def _():
        def clear(j, carry):
            k_all[j] = jnp.zeros((TOK, cw), BF16)
            v_all[j] = jnp.zeros((TOK, cw), BF16)
            r_all[j] = jnp.zeros((8, 128), F32)
            id_all[j] = jnp.full((8, 128), -1.0, F32)
            return carry

        lax.fori_loop(0, width, clear, 0)

    own_k = pltpu.make_async_copy(att_k.at[:, lanes(w, cw)], k_all.at[width + w], loc_sem.at[0])
    own_q = pltpu.make_async_copy(att_q.at[:, lanes(w, cw)], q_all.at[w], loc_sem.at[1])
    own_k.start()
    own_q.start()

    loaded(ids)
    id_row = ids[...].astype(F32)
    id_send[...] = jnp.broadcast_to(id_row, (8, 128))
    id_all[width + w] = jnp.broadcast_to(id_row, (8, 128))
    idc[TOK:] = jnp.broadcast_to(id_row, (TOK, 128)).T
    loaded(se_k, se_v)
    sh_send[...] = (se_k[TOK - 16 :, :].astype(F32) * se_v[TOK - 16 :, :].astype(F32)).astype(BF16)

    def local_part(g, carry):
        col = lanes(g)
        row = lax.broadcasted_iota(jnp.int32, (MR_K, 128), 0).astype(F32)
        filt[:, col] = mr_taps[:, col].astype(F32) * jnp.exp(-(rates[:, col] * row))
        ue[TOK:, col] = (
            (se_k[:, col].astype(F32) * se_v[:, col].astype(F32)).astype(BF16).astype(F32)
        )
        return carry

    def filter_part(g, carry):
        col = lanes(g, 256)
        full = filt[:, col]
        high = full.astype(BF16)
        low = (full - high.astype(F32)).astype(BF16)
        hat = jnp.dot(forth[...], high, preferred_element_type=F32) + jnp.dot(
            forth[...], low, preferred_element_type=F32
        )
        top = lax.broadcasted_iota(jnp.int32, (TOK, 256), 0) == 0
        hat_a[:, col] = hat[:TOK]
        hat_b[:, col] = jnp.where(top, 0.0, hat[TOK:])
        hat_c[:, col] = jnp.where(top, hat[TOK:], hat[:TOK])
        return carry

    loaded(mr_taps, rates, forth)
    lax.fori_loop(0, groups, local_part, 0)
    lax.fori_loop(0, groups // 2, filter_part, 0)
    idc[:TOK] = jnp.full((TOK, 128), -1.0, F32)
    ue[TOK - 8 : TOK, :] = jnp.zeros((8, chans), F32)
    here = idc[TOK:]
    for tap in range(1, SE_K):
        m7[tap] = (idc[TOK - tap : 2 * TOK - tap] == here).astype(F32)
    sq[...] = jnp.zeros_like(sq)

    def short_rows(start, size, col):
        rows = slice(start, start + size)
        acc = ue[TOK + start : TOK + start + size, col] * se_taps[0:1, col]
        for tap in range(1, SE_K):
            acc += (ue[TOK + start - tap : TOK + start + size - tap, col] * m7[tap, rows, :]) * se_taps[
                tap : tap + 1, col
            ]
        out = se_q[rows, col].astype(F32) * acc
        sq[rows, :] += out * out
        out = out * se_gain[:, col]
        ybuf[rows, col] = out
        v_send[rows, col] = (out * mr_k[rows, col].astype(F32)).astype(BF16)

    def short_part(g, carry):
        for rb in range(TOK // 32):
            short_rows(32 * rb, 32, lanes(g))
        return carry

    blocks = TOK // 16

    def masks(a, carry):
        base = pl.multiple_of(a * 16, 16)
        first = idc[pl.ds(base + TOK, 8), :][0:1, :]
        ma[a] = (idc[TOK:, :] == first).astype(F32)
        ul[...] = idc[pl.ds(base + TOK - 16, 32), :]
        sub = lax.broadcasted_iota(jnp.int32, (8, 128), 0)
        at = 0
        for tile in range(2):
            mine = ul[16 + 8 * tile : 24 + 8 * tile, :]
            for tap in range(8 * tile + 8):
                then = ul[16 + 8 * tile - tap : 24 + 8 * tile - tap, :]
                keep = (mine == then) & (mine != first) & (sub + 8 * tile >= tap)
                mb[a, at] = keep.astype(F32)
                at += 1
        return carry

    lax.fori_loop(0, blocks, masks, 0)
    um[...] = jnp.zeros_like(um)

    loaded(se_q, mr_k, se_taps, se_gain)
    lax.fori_loop(0, groups, short_part, 0)

    pl.semaphore_wait(barrier, (width - 1) + 2 + (mps - 1))

    id_next = remote(id_send, id_prev, h_ss.at[0], h_rs.at[0], next_seq)
    id_next.start()
    sh_next = remote(sh_send, sh_recv, h_ss.at[1], h_rs.at[1], next_seq)
    sh_next.start()
    sends = [id_next, sh_next]
    halo = [
        remote(v_send.at[rows], v_recv.at[rows], h_ss.at[at], h_rs.at[at], next_seq)
        for at, rows in ((3, pl.ds(16, TOK - 16)), (4, pl.ds(0, 16)))
    ]
    sends += halo
    halo[0].start()
    for step in range(1, width):
        there = ring(w, step, width)
        copy = remote(
            id_send, id_all.at[width + w], i_ss.at[step], i_rs.at[w], {"seq": mate(step)}
        )
        copy.start()
        sends.append(copy)
        copy = remote(
            att_k.at[:, lanes(there, cw)],
            k_all.at[width + w],
            k_ss.at[step],
            k_rs.at[w],
            {"seq": mate(step)},
        )
        copy.start()
        sends.append(copy)

    id_next.wait_recv()
    idc[:TOK] = jnp.broadcast_to(id_prev[0:1, :], (TOK, 128)).T
    for tap in range(1, SE_K):
        m7[tap, 0:16] = (idc[TOK - tap : TOK + 16 - tap] == idc[TOK : TOK + 16]).astype(F32)
    sh_next.wait_recv()
    ue[TOK - 8 : TOK, :] = sh_recv[...].astype(F32)[8:16, :]
    sq[0:16, :] = jnp.zeros((16, 128), F32)

    def first_rows(g, carry):
        short_rows(0, 16, lanes(g))
        return carry

    lax.fori_loop(0, groups, first_rows, 0)
    halo[1].start()

    def psum_start(which):
        row = jnp.sum(sq[...].T, axis=0, keepdims=True)
        ps_send[which] = jnp.broadcast_to(row, (8, 128))
        copies = []
        for step in range(1, mps):
            copy = remote(
                ps_send.at[which],
                ps_recv.at[which, step],
                ps_ss.at[which, step],
                ps_rs.at[which, step],
                {"mp": ring(mp, step, mps)},
            )
            copy.start()
            copies.append(copy)
        return copies

    def psum_end(which, copies):
        total = ps_send[which]
        for step, copy in enumerate(copies, 1):
            copy.wait_recv()
            total = total + ps_recv[which, step]
        return lax.rsqrt(total / d_model + 1e-06)

    def column(rows8):
        return jnp.broadcast_to(rows8[0:1, :], (TOK, 128)).T

    copies = psum_start(0)
    sends += copies

    m_prior[...] = (idc[:TOK] == idc[TOK : TOK + 1, :]).astype(F32)
    r_own = psum_end(0, copies)
    r_send[...] = r_own
    r_next = remote(r_send, r_recv, h_ss.at[2], h_rs.at[2], next_seq)
    r_next.start()
    sends.append(r_next)
    r_col[...] = column(r_own)

    def medium_part(g, carry):
        col = lanes(g)
        se_out = (ybuf[:, col] * r_col[...]).astype(BF16).astype(F32)
        ue[TOK:, col] = (mr_k[:, col].astype(F32) * se_out).astype(BF16).astype(F32)
        for a in range(blocks):
            size = 16 * a + 16
            base = 16 * a
            win = um.at[a % 2]
            win[8 : 8 + size, :] = ue[TOK : TOK + size, col] * ma[a, 0:size, :]
            acc = [[jnp.zeros((8, 128), F32) for _ in range(4)] for _ in range(2)]
            for phase in range(8):
                wins = [win[8 + 8 * k - phase : 16 + 8 * k - phase, :] for k in range(2 * a + 2)]
                for m in range(2 * a + 2):
                    tap = filt[8 * m + phase : 8 * m + phase + 1, col]
                    for tile in range(2):
                        if 2 * a + tile >= m:
                            acc[tile][phase % 4] += wins[2 * a + tile - m] * tap
            at = 0
            for tile in range(2):
                row = base + 8 * tile
                total = (acc[tile][0] + acc[tile][1]) + (acc[tile][2] + acc[tile][3])
                total = total * ma[a, row : row + 8, :]
                for tap in range(8 * tile + 8):
                    total += (
                        ue[TOK + row - tap : TOK + row + 8 - tap, col] * mb[a, at]
                    ) * filt[tap : tap + 1, col]
                    at += 1
                ybuf[row : row + 8, col] = total
        return carry

    def relay_key(src):
        return remote(k_all.at[width + src], k_all.at[src], kf_ss.at[src], kf_rs.at[src], next_plane)

    id_up = remote(
        id_all.at[pl.ds(width, width)], id_all.at[pl.ds(0, width)], if_ss.at[0], if_rs.at[0], next_plane
    )

    def medium_and_relay(g, carry):
        medium_part(g, carry)
        i = g - relay_from
        src = ring(w, -i, width)

        @pl.when(i != 0)
        def _():
            slot = width + src
            remote(k_all.at[slot], k_all.at[slot], k_ss.at[0], k_rs.at[src], next_seq).wait_recv()
            remote(id_all.at[slot], id_all.at[slot], i_ss.at[0], i_rs.at[src], next_seq).wait_recv()

        @pl.when(z < planes - 1)
        def _():
            relay_key(src).start()

        return carry

    relay_from = groups - width
    lax.fori_loop(0, relay_from, medium_part, 0)
    own_k.wait()
    lax.fori_loop(relay_from, groups, medium_and_relay, 0)
    pl.when(z < planes - 1)(id_up.start)

    loaded(mr_q, mr_gain, att_gain, back)
    r_next.wait_recv()
    r_col[...] = column(r_recv[...]) * m_prior[...]
    for copy in halo:
        copy.wait_recv()
    for step in range(1, width):
        there = ring(w, step, width)
        copy = remote(
            att_q.at[:, lanes(there, cw)], q_all.at[w], q_ss.at[step], q_rs.at[w], {"seq": mate(step)}
        )
        copy.start()
        sends.append(copy)
    sq[...] = jnp.zeros_like(sq)

    def prior_part(g, carry):
        wide = lanes(g, 256)
        halves = [lanes(2 * g + half) for half in range(2)]
        factor = r_col[...]
        for half, col in enumerate(halves):
            u_in[:, 128 * half : 128 * half + 128] = (v_recv[:, col].astype(F32) * factor).astype(BF16)
        hat[...] = jnp.dot(forth[...], u_in[...], preferred_element_type=F32)
        hat_y[:TOK, :] = (hat[:TOK] * hat_a[:, wide] - hat[TOK:] * hat_b[:, wide]).astype(BF16)
        hat_y[TOK:, :] = (hat[:TOK] * hat_b[:, wide] + hat[TOK:] * hat_c[:, wide]).astype(BF16)
        prior = jnp.dot(back[...], hat_y[...], preferred_element_type=F32)
        keep = ma[0]
        for half, col in enumerate(halves):
            out = ybuf[:, col] + keep * prior[:, 128 * half : 128 * half + 128]
            out = mr_q[:, col].astype(F32) * out
            ybuf[:, col] = out
            sq[...] += out * out
        return carry

    lax.fori_loop(0, groups // 2, prior_part, 0)

    copies = psum_start(1)
    sends += copies

    def raw_chunk(there):
        for part in range(cw // 128):
            col = lanes(there * (cw // 128) + part)
            v_raw[:, col] = (ybuf[:, col] * mr_gain[:, col]).astype(BF16)

    for step in range(1, width):
        there = ring(w, step, width)
        raw_chunk(there)
        copy = remote(
            v_raw.at[:, lanes(there, cw)], v_all.at[width + w], v_ss.at[step], v_rs.at[w], {"seq": mate(step)}
        )
        copy.start()
        sends.append(copy)
    raw_chunk(w)
    own_v = pltpu.make_async_copy(v_raw.at[:, lanes(w, cw)], v_all.at[width + w], loc_sem.at[2])
    own_v.start()

    r_own = psum_end(1, copies)
    r_val[...] = r_own
    r_all[width + w] = r_own
    for step in range(1, width):
        copy = remote(r_val, r_all.at[width + w], g_ss.at[step], g_rs.at[w], {"seq": mate(step)})
        copy.start()
        sends.append(copy)
    r_col[...] = column(r_own)

    own_q.wait()
    for step in range(1, width):
        src = ring(w, -step, width)
        remote(q_all.at[src], q_all.at[src], q_ss.at[step], q_rs.at[src], next_seq).wait_recv()

    def take_keys(src, carry):
        @pl.when(z > 0)
        def _():
            relay_key(src).wait_recv()

        return carry

    lax.fori_loop(0, width, take_keys, 0)
    pl.when(z > 0)(id_up.wait_recv)

    scale = HEAD**-0.5 * math.log2(math.e)
    tri = lax.broadcasted_iota(jnp.int32, (TOK, TOK), 0) >= lax.broadcasted_iota(
        jnp.int32, (TOK, TOK), 1
    )

    def weights(b):
        id_q = column(id_all[width + b])
        for h in range(heads):
            hl = slice(h * HEAD, (h + 1) * HEAD)
            q = q_all[b, :, hl]
            top = None
            for kk in range(span):
                s = lax.dot_general(
                    q,
                    k_all[b + kk, :, hl],
                    (((1,), (1,)), ((), ())),
                    preferred_element_type=F32,
                )
                keep = id_q == jnp.broadcast_to(id_all[b + kk][0:1, :], (TOK, TOK))
                if kk == span - 1:
                    keep = keep & tri
                s = jnp.where(keep, s * scale, -1e30)
                s_buf[kk] = s
                top = s if top is None else jnp.maximum(top, s)
            top = jnp.max(top, axis=1, keepdims=True)
            total = None
            for kk in range(span):
                e = jnp.exp2(s_buf[kk] - top)
                total = e if total is None else total + e
                p_all[b, h, :, kk * TOK : (kk + 1) * TOK] = e.astype(BF16)
            total = jnp.sum(total, axis=1, keepdims=True)
            linv[b, h] = jnp.broadcast_to(1.0 / total, (TOK, TOK))

    own_v.wait()

    def relay_value(src):
        return remote(v_all.at[width + src], v_all.at[src], f_ss.at[src], f_rs.at[src], next_plane)

    r_up = remote(
        r_all.at[pl.ds(width, width)], r_all.at[pl.ds(0, width)], gf_ss.at[0], gf_rs.at[0], next_plane
    )

    def weigh(i, carry):
        src = ring(w, -i, width)
        slot = width + src

        @pl.when(i != 0)
        def _():
            remote(v_all.at[slot], v_all.at[slot], v_ss.at[0], v_rs.at[src], next_seq).wait_recv()

        @pl.when(z < planes - 1)
        def _():
            relay_value(src).start()

        weights(i)
        return carry

    lax.fori_loop(0, width, weigh, 0)

    def norm_out(g, carry):
        col = lanes(g)
        mr_out[:, col] = (ybuf[:, col] * r_col[...] * mr_gain[:, col]).astype(BF16)
        return carry

    lax.fori_loop(0, groups, norm_out, 0)

    def scale_values(slot):
        factor = column(r_all[slot])
        for part in range(cw // 128):
            col = slice(part * 128, (part + 1) * 128)
            v_s[slot, :, col] = (v_all[slot, :, col].astype(F32) * factor).astype(BF16)

    def take_factor(i, carry):
        src = ring(w, -i, width)
        slot = width + src
        remote(r_all.at[slot], r_all.at[slot], g_ss.at[0], g_rs.at[src], next_seq).wait_recv()
        return carry

    lax.fori_loop(1, width, take_factor, 0)
    pl.when(z < planes - 1)(r_up.start)

    def take_own(i, carry):
        scale_values(width + i)
        return carry

    lax.fori_loop(0, width, take_own, 0)

    for b in range(width):
        for h in range(heads):
            hl = slice(h * HEAD, (h + 1) * HEAD)
            o_acc[b, h] = jnp.dot(
                p_all[b, h, :, (width - b) * TOK :],
                v_s[width : width + b + 1, :, hl].reshape((b + 1) * TOK, HEAD),
                preferred_element_type=F32,
            )

    for b in range(width - 1, -1, -1):
        @pl.when(z > 0)
        def _():
            relay_value(b).wait_recv()
            if b == width - 1:
                r_up.wait_recv()

        scale_values(b)
        squares = None
        for h in range(heads):
            hl = slice(h * HEAD, (h + 1) * HEAD)
            o = o_acc[b, h] + jnp.dot(
                p_all[b, h, :, : (width - b) * TOK],
                v_s[b:width, :, hl].reshape((width - b) * TOK, HEAD),
                preferred_element_type=F32,
            )
            o = o * linv[b, h]
            o_send[b, :, hl] = o.astype(BF16)
            squares = o * o if squares is None else squares + o * o

        @pl.when(w != b)
        def _():
            remote(
                o_send.at[b],
                o_all.at[w],
                o_ss.at[b],
                o_rs.at[w],
                {"seq": z * width + b},
            ).start()

        ps_send[2, b : b + 1, :] = jnp.sum(squares.T, axis=0, keepdims=True)

    copies = []
    for step in range(1, mps):
        copy = remote(
            ps_send.at[2],
            ps_recv.at[2, step],
            ps_ss.at[2, step],
            ps_rs.at[2, step],
            {"mp": ring(mp, step, mps)},
        )
        copy.start()
        copies.append(copy)
    sends += copies
    o_all[w] = o_send[w]
    total = ps_send[2]
    for step, copy in enumerate(copies, 1):
        copy.wait_recv()
        total = total + ps_recv[2, step]
    t_val[...] = total
    t_all[w] = total
    for step in range(1, width):
        copy = remote(t_val, t_all.at[w], t_ss.at[step], t_rs.at[w], {"seq": mate(step)})
        copy.start()
        sends.append(copy)

    def collect(i, total):
        src = ring(w, i, width)

        @pl.when(i != 0)
        def _():
            remote(t_all.at[src], t_all.at[src], t_ss.at[0], t_rs.at[src], next_seq).wait_recv()

        return total + t_all[src]

    t_val2[...] = lax.fori_loop(0, width, collect, jnp.zeros((8, 128), F32))
    mine = t_val2[pl.ds(w, 1), :]
    scale_col = jnp.broadcast_to(lax.rsqrt(mine / d_model + 1e-06), (TOK, 128)).T

    def finish(i, carry):
        src = ring(w, i, width)

        @pl.when(i != 0)
        def _():
            remote(o_all.at[src], o_all.at[src], o_ss.at[src], o_rs.at[src], next_seq).wait_recv()

        for part in range(cw // 128):
            col = lanes(src * (cw // 128) + part)
            out = o_all[src, :, part * 128 : (part + 1) * 128].astype(F32)
            att_out[:, col] = (out * scale_col * att_gain[:, col]).astype(BF16)
        return carry

    lax.fori_loop(0, width, finish, 0)

    for copy in sends:
        copy.wait_send()

    def drain(j, carry):
        @pl.when(z < planes - 1)
        def _():
            relay_key(j).wait_send()
            relay_value(j).wait_send()
        @pl.when(j != w)
        def _():
            remote(
                o_send.at[j], o_all.at[w], o_ss.at[j], o_rs.at[w], {"seq": z * width + j}
            ).wait_send()

        return carry

    lax.fori_loop(0, width, drain, 0)

    @pl.when(z < planes - 1)
    def _():
        id_up.wait_send()
        r_up.wait_send()


def local(planes, width, mps, d_model, *args):
    (se_q, se_k, se_v, mr_q, mr_k, att_q, att_k, ids, se_taps, mr_taps, rates, g1, g2, g3) = args
    chans = se_q.shape[1]
    cw = chans // width
    heads = cw // HEAD
    span = width + 1
    vm = pl.BlockSpec(memory_space=pltpu.VMEM)
    hbm = pl.BlockSpec(memory_space=pl.ANY)
    vmem = pltpu.VMEM
    dma = pltpu.SemaphoreType.DMA
    out = jax.ShapeDtypeStruct((TOK, chans), BF16)
    return pl.pallas_call(
        functools.partial(kernel, planes, width, mps, d_model),
        out_shape=(out, out),
        in_specs=[hbm] * 16,
        out_specs=(vm, vm),
        scratch_shapes=[
            vmem((TOK, chans), BF16),
            vmem((TOK, chans), BF16),
            vmem((TOK, chans), BF16),
            vmem((TOK, chans), BF16),
            vmem((TOK, chans), BF16),
            vmem((1, TOK), jnp.int32),
            vmem((SE_K, chans), F32),
            vmem((MR_K, chans), BF16),
            vmem((1, chans), F32),
            vmem((1, chans), F32),
            vmem((1, chans), F32),
            vmem((1, chans), F32),
            vmem((2 * TOK, TOK), BF16),
            vmem((TOK, 2 * TOK), BF16),
            dma((14,)),
            vmem((2 * TOK, chans), F32),
            vmem((TOK, chans), F32),
            vmem((MR_K, chans), F32),
            vmem((2 * TOK, 128), F32),
            vmem((SE_K, TOK, 128), F32),
            vmem((TOK // 16, TOK, 128), F32),
            vmem((TOK // 16, 24, 8, 128), F32),
            vmem((2, TOK + 8, 128), F32),
            vmem((32, 128), F32),
            vmem((TOK, 128), F32),
            vmem((16, chans), BF16),
            vmem((16, chans), BF16),
            vmem((TOK, chans), BF16),
            vmem((TOK, chans), BF16),
            vmem((8, 128), F32),
            vmem((8, 128), F32),
            vmem((3, 8, 128), F32),
            vmem((3, mps, 8, 128), F32),
            vmem((8, 128), F32),
            vmem((8, 128), F32),
            vmem((2 * width, 8, 128), F32),
            vmem((2 * width, TOK, cw), BF16),
            vmem((width, TOK, cw), BF16),
            vmem((2 * width, TOK, cw), BF16),
            vmem((span, TOK, TOK), F32),
            vmem((width, heads, TOK, span * TOK), BF16),
            vmem((width, heads, TOK, TOK), F32),
            vmem((TOK, chans), BF16),
            vmem((2 * width, TOK, cw), BF16),
            vmem((TOK, chans), F32),
            vmem((TOK, chans), F32),
            vmem((TOK, chans), F32),
            vmem((2 * TOK, 256), F32),
            vmem((2 * TOK, 256), BF16),
            vmem((TOK, 256), BF16),
            vmem((TOK, 128), F32),
            vmem((TOK, 128), F32),
            vmem((width, heads, TOK, HEAD), F32),
            vmem((8, 128), F32),
            vmem((8, 128), F32),
            vmem((width, 8, 128), F32),
            vmem((8, 128), F32),
            vmem((2 * width, 8, 128), F32),
            vmem((width, TOK, cw), BF16),
            vmem((width, TOK, cw), BF16),
            dma((3,)),
            dma((width,)),
            dma((width,)),
            dma((width,)),
            dma((width,)),
            dma((width,)),
            dma((width,)),
            dma((width,)),
            dma((width,)),
            dma((width,)),
            dma((width,)),
            dma((width,)),
            dma((width,)),
            dma((width,)),
            dma((width,)),
            dma((width,)),
            dma((width,)),
            dma((1,)),
            dma((1,)),
            dma((1,)),
            dma((1,)),
            dma((width,)),
            dma((width,)),
            dma((3, mps)),
            dma((3, mps)),
            dma((8,)),
            dma((8,)),
        ],
        compiler_params=pltpu.CompilerParams(
            collective_id=0, has_side_effects=True, vmem_limit_bytes=60 * 1024 * 1024
        ),
    )(
        se_q,
        se_k,
        se_v,
        mr_q,
        mr_k,
        att_q,
        att_k,
        ids.reshape(1, TOK),
        se_taps,
        mr_taps,
        rates.reshape(1, chans),
        g1.reshape(1, chans),
        g2.reshape(1, chans),
        g3.reshape(1, chans),
        *transforms(TOK),
    )


def solution(mesh, width=8, d_model=D):
    planes = mesh.shape["seq"] // width
    spec = P("seq", "mp")
    return jax.shard_map(
        functools.partial(local, planes, width, mesh.shape["mp"], d_model),
        mesh=mesh,
        in_specs=(spec,) * 7
        + (P("seq"), P(None, "mp"), P(None, "mp"), P("mp"), P("mp"), P("mp"), P("mp")),
        out_specs=(spec, spec),
        check_vma=False,
    )
```
